32 devices in a mesh: pair: 8 (over z, y), aux: 4 (over x, core).
Axes of the slice: x: 2, y: 2, z: 4, core: 2. Of those that a mesh axis runs over, the one named last changes fastest.
Arguments:
- factors: bfloat16 [8, 8192, 8, 128], P('pair', 'aux'), may hold values from -0.0625 to 0.0625
- amplitudes: bfloat16 [48, 128, 128], P('pair'), may hold values from -20 to 20
- block_list: int32 [48, 3], P('pair'), may hold values from 0 to 7, as said below
- owner_map: int32 [8], replicated, may hold values from 0 to 7, as said below
Outputs:
- residual_blocks: bfloat16 [48, 128, 128], P('pair')
The draws below stay inside these ranges and needn't reach their ends.
Inputs may be any that keep to these rules, and one draw needn't show every extreme that they name: `block_list`: each row (k, A, C) names an occupied orbital below 8 and two virtual blocks below 8; no row repeats. Among the 6 rows of one device at most 2 have orbitals with the same owner_map entry, and exactly 2 for some entry on every device. `owner_map`: A permutation: entry k is the row of factors that holds orbital k.
All inputs are finite; a program needn't handle non-finite values.
Results may differ from the reference program's by a relative error of at most 0.0046.
Values may be sent and summed in bfloat16 or wider, within the bound.
No kernel may reach another device: no remote copies, remote signals or barrier semaphores. Data moves between devices by JAX's collectives and lax.ppermute only.
A program may use at most 64 MiB of HBM per device.

```python
import jax
import jax.numpy as jnp
from jax import lax

VB = 128
NV = 8
NAUX = 8192
NO = 8
BLK_DEV = 6
NBLK = 48
N_PAIR = 8


def common_layout(key):
    return jax.random.permutation(jax.random.fold_in(key, 11), NO).astype(jnp.int32)


def draw_owner_map(key, part):
    return common_layout(key)


def draw_block_list(key, part):
    owner_table = common_layout(key)
    orbital_at = jnp.argsort(owner_table).astype(jnp.int32)
    senders = jnp.arange(N_PAIR, dtype=jnp.int32)
    distances = jnp.arange(N_PAIR, dtype=jnp.int32)
    scores = jax.random.permutation(jax.random.fold_in(key, 17), N_PAIR).astype(jnp.int32)
    special = (distances == N_PAIR // 2) | (distances == N_PAIR - 1) | (distances == 1)
    priority = scores + jnp.where(special, -2 * N_PAIR, 0)
    reach_set = jnp.argsort(priority)[:BLK_DEV // 2].astype(jnp.int32)
    pick_key = jax.random.fold_in(key, 23)
    chosen = jax.vmap(lambda sender: jax.random.permutation(jax.random.fold_in(pick_key, sender), BLK_DEV))(senders)
    chosen = chosen.astype(jnp.int32)
    ranks = chosen // 2
    offsets = reach_set[ranks]
    owners = (senders[:, None] - offsets) % N_PAIR
    combos = chosen
    table_key = jax.random.fold_in(key, 37)
    tables = jax.vmap(lambda owner: jax.random.permutation(jax.random.fold_in(table_key, owner), NV * NV))(senders)
    tables = tables.astype(jnp.int32)
    codes = tables[owners, combos]
    block_a = codes // NV
    block_c = codes % NV
    orbitals = orbital_at[owners]
    listed = jnp.stack([orbitals, block_a, block_c], axis=-1)
    return listed.reshape(N_PAIR * BLK_DEV, 3).astype(jnp.int32)


def block_levels(stream_key, shape, split, least, high):
    def one(dim, parts):
        heights = jax.random.uniform(jax.random.fold_in(jax.random.fold_in(stream_key, 6), dim), (parts,), jnp.float32, least / len(split), high / len(split))
        return jnp.repeat(jnp.exp(heights), shape[dim] // parts).reshape((-1,) + (1,) * (len(shape) - dim - 1))

    level = one(*split[0])
    for cut in split[1:]:
        level = level * one(*cut)
    return level


def scatter_about(own_key, shape, scale, most, cuts=(), kind=jnp.bfloat16):
    entries = scale * jax.random.normal(own_key, shape, jnp.float32)
    if cuts:
        entries = entries * block_levels(own_key, shape, cuts, -0.22, 0.18)
    return jnp.clip(entries, -most, most).astype(kind)


def setup_inputs(seed: int = 0) -> dict:
    streams_of = jax.random.split(jax.random.key(seed), 5)
    factors = scatter_about(streams_of[0], (NO, NAUX, NV, VB), NAUX ** -0.5, 0.0625, ((0, 8), (1, 4)))
    amplitudes = scatter_about(streams_of[1], (NBLK, VB, VB), ((NAUX * NV / (BLK_DEV * N_PAIR * VB)) ** 0.5), 20.0, ((0, 8),))
    block_list = draw_block_list(jax.random.fold_in(streams_of[4], 71), 0)
    owner_map = draw_owner_map(jax.random.fold_in(streams_of[4], 71), 0)
    return dict(factors=factors, amplitudes=amplitudes, block_list=block_list, owner_map=owner_map)


def reference(factors, amplitudes, block_list, owner_map):
    orbitals = block_list[:, 0].astype(jnp.int32)
    block_a = block_list[:, 1].astype(jnp.int32)
    block_c = block_list[:, 2].astype(jnp.int32)
    rows = owner_map[orbitals].astype(jnp.int32)
    flipped = jnp.transpose(amplitudes.astype(jnp.float32), (0, 2, 1))
    placed = jnp.zeros((NO, NV, VB, NV, VB), jnp.float32).at[rows, block_c, :, block_a, :].add(flipped)
    placed = placed.reshape(NO, NV * VB, NV * VB)
    wide_factors = factors.astype(jnp.float32).reshape(NO, NAUX, NV * VB)

    def accumulate_rows(running, inputs):
        factor_rows, weights = inputs
        return running + jnp.dot(factor_rows, weights, preferred_element_type=jnp.float32), None

    start_total = jnp.zeros((NAUX, NV * VB), jnp.float32)
    summed, unused = lax.scan(accumulate_rows, start_total, (wide_factors, placed))
    inter = summed.astype(jnp.bfloat16).astype(jnp.float32)

    def project_rows(carry, factor_rows):
        return carry, jnp.dot(inter.T, factor_rows, preferred_element_type=jnp.float32)

    unused_carry, projected = lax.scan(project_rows, jnp.zeros((), jnp.float32), wide_factors)
    projected = projected.reshape(NO, NV, VB, NV, VB)
    picked = projected[rows, block_a, :, block_c, :]
    return picked.astype(jnp.bfloat16)
```

```python
import jax
import jax.numpy as jnp
from jax import lax
from jax.experimental import pallas as pl
from jax.experimental.pallas import tpu as pltpu
from jax.sharding import PartitionSpec as P

RANKS = 2
GROUP = 48
META = 16
SMALL = 16
VMEM_BYTES = 40 * 1024 * 1024

SMEM_SPEC = pl.BlockSpec(memory_space=pltpu.SMEM)
VMEM_SPEC = pl.BlockSpec(memory_space=pltpu.VMEM)
PARAMS = pltpu.CompilerParams(vmem_limit_bytes=VMEM_BYTES)


def pack_kernel(slots, bits, place_ref, list_ref, owner_ref, blocks_ref, out_ref, pos_ref, meta_ref):
    group = place_ref[0]
    half = place_ref[1]
    count, width, depth = blocks_ref.shape
    rows = width // 2
    out_ref[...] = jnp.zeros_like(out_ref)
    meta_ref[...] = jnp.zeros_like(meta_ref)
    line = lax.broadcasted_iota(jnp.int32, meta_ref.shape[1:], 0)
    lane = lax.broadcasted_iota(jnp.int32, meta_ref.shape[1:], 1)

    def place(j, carry):
        owner = owner_ref[list_ref[j, 0]]

        def earlier(i, total):
            same = (owner_ref[list_ref[i, 0]] >> bits) == (owner >> bits)
            return total + same.astype(jnp.int32)

        slot = lax.fori_loop(0, j, earlier, jnp.int32(0))
        hop = (owner >> bits) ^ group
        pos_ref[j] = hop * slots + slot
        start = pl.multiple_of(slot * rows, rows)
        taken = pl.ds(pl.multiple_of(half * rows, rows), rows)
        out_ref[hop, pl.ds(start, rows), :] = blocks_ref[j, taken, :]
        is_line = line == slot
        old = meta_ref[hop]
        local = owner & ((1 << bits) - 1)
        for k, value in enumerate((list_ref[j, 1], list_ref[j, 2], local)):
            old = jnp.where(is_line & (lane == k), (value + 1).astype(jnp.float32), old)
        meta_ref[hop] = old
        return carry

    lax.fori_loop(0, count, place, 0)
    out_ref[:, pl.ds(slots * rows, META), :] = meta_ref[...].astype(out_ref.dtype)


def pack(place, block_list, owner_map, blocks, slots, bits, groups):
    count, width, depth = blocks.shape
    height = slots * (width // 2) + META
    return pl.pallas_call(
        lambda *refs: pack_kernel(slots, bits, *refs),
        out_shape=(
            jax.ShapeDtypeStruct((groups, height, depth), blocks.dtype),
            jax.ShapeDtypeStruct((count,), jnp.int32),
        ),
        in_specs=[SMEM_SPEC, SMEM_SPEC, SMEM_SPEC, VMEM_SPEC],
        out_specs=(VMEM_SPEC, SMEM_SPEC),
        scratch_shapes=[pltpu.VMEM((groups, META, depth), jnp.float32)],
        compiler_params=PARAMS,
        name="pack",
    )(place, block_list, owner_map, blocks)


def unpack_kernel(slots, where_ref, mine_ref, out_ref):
    step = pl.program_id(0)
    rows = out_ref.shape[1] // 2
    out_ref[...] = jnp.zeros_like(out_ref)
    for slot in range(slots):
        odd = where_ref[0, step * slots + slot] & 1
        there = pl.ds(pl.multiple_of(odd * rows, rows), rows)
        out_ref[slot, there, :] = mine_ref[0, slot * rows : (slot + 1) * rows, :]


def unpack(where, mine, slots):
    pairs, height, depth = mine.shape
    width = (height - META) // slots * 2
    return pl.pallas_call(
        lambda *refs: unpack_kernel(slots, *refs),
        grid=(pairs,),
        out_shape=jax.ShapeDtypeStruct((pairs * slots, width, depth), mine.dtype),
        in_specs=[SMEM_SPEC, pl.BlockSpec((1, height, depth), lambda i: (i, 0, 0))],
        out_specs=pl.BlockSpec((slots, width, depth), lambda i: (i, 0, 0)),
        compiler_params=PARAMS,
        name="unpack",
    )(where, mine)


def contract_kernel(group, where_ref, blocks_ref, factors_ref, out_ref, sent_ref):
    step = pl.program_id(0)

    @pl.when(step == 0)
    def _():
        out_ref[...] = jnp.zeros_like(out_ref)

    def one(i, carry):
        a = where_ref[0, step * group + i]

        @pl.when(a >= 0)
        def _():
            f = where_ref[1, step * group + i]
            out_ref[a >> 1] += lax.dot_general(
                factors_ref[f],
                blocks_ref[i],
                (((1,), (1,)), ((), ())),
                preferred_element_type=jnp.float32,
            )

        return carry

    lax.fori_loop(0, group, one, 0)

    @pl.when(step == pl.num_programs(0) - 1)
    def _():
        sent_ref[...] = out_ref[...].astype(sent_ref.dtype)


def contract(where, blocks, factors, virt):
    slots, width, depth = blocks.shape
    height = factors.shape[1]
    group = min(GROUP, slots)
    shape = (virt // 2, height, width)
    whole = pl.BlockSpec(shape, lambda i: (0, 0, 0))
    return pl.pallas_call(
        lambda *refs: contract_kernel(group, *refs),
        grid=(slots // group,),
        out_shape=(
            jax.ShapeDtypeStruct(shape, jnp.float32),
            jax.ShapeDtypeStruct(shape, jnp.bfloat16),
        ),
        in_specs=[
            SMEM_SPEC,
            pl.BlockSpec((group, width, depth), lambda i: (i, 0, 0)),
            pl.BlockSpec(factors.shape, lambda i: (0, 0, 0)),
        ],
        out_specs=(whole, whole),
        compiler_params=PARAMS,
        name="contract",
    )(where, blocks, factors)


def project_kernel(group, first, where_ref, own_ref, got_ref, factors_ref, *refs):
    out_ref, inter_ref = refs[-2:]
    step = pl.program_id(0)
    rows = out_ref.shape[1]

    @pl.when(step == 0)
    def _():
        whole = own_ref[...] + got_ref[...].astype(jnp.float32)
        inter_ref[...] = whole.astype(inter_ref.dtype)

    if first:
        out_ref[...] = jnp.zeros_like(out_ref)
    else:
        out_ref[...] = refs[0][...]

    def one(i, carry):
        a = where_ref[0, step * group + i]

        @pl.when(a >= 0)
        def _():
            f = where_ref[1, step * group + i]
            term = lax.dot_general(
                inter_ref[a >> 1],
                factors_ref[f],
                (((0,), (0,)), ((), ())),
                preferred_element_type=jnp.float32,
            )
            out_ref[i] += jnp.where((a & 1) == 0, term[:rows], term[rows:])

        return carry

    lax.fori_loop(0, group, one, 0)


def project(where, own, got, factors, so_far):
    slots = where.shape[1]
    width, depth = own.shape[2], factors.shape[2]
    group = min(GROUP, slots)
    first = so_far is None
    block = pl.BlockSpec((group, width // 2, depth), lambda i: (i, 0, 0))
    whole = pl.BlockSpec(own.shape, lambda i: (0, 0, 0))
    return pl.pallas_call(
        lambda *refs: project_kernel(group, first, *refs),
        grid=(slots // group,),
        out_shape=jax.ShapeDtypeStruct((slots, width // 2, depth), jnp.float32),
        in_specs=[SMEM_SPEC, whole, whole, pl.BlockSpec(factors.shape, lambda i: (0, 0, 0))]
        + ([] if first else [block]),
        out_specs=block,
        scratch_shapes=[pltpu.VMEM(own.shape, jnp.bfloat16)],
        input_output_aliases={} if first else {4: 0},
        compiler_params=PARAMS,
        name="project",
    )(where, own, got, factors, *([] if first else [so_far]))


def on_device(factors, amplitudes, block_list, owner_map):
    pairs = lax.axis_size("pair")
    shares = lax.axis_size("aux")
    small = pairs <= SMALL
    members = 4 if small else 2
    chunks = 4 if small else 1
    bits = members.bit_length() - 1
    groups = pairs // members
    wide = shares // 2
    me = lax.axis_index("pair")
    share = lax.axis_index("aux")
    local, team = me & (members - 1), me >> bits
    half, part = share & 1, share >> 1
    place = jnp.stack([team, half]).astype(jnp.int32)
    count, width, depth = amplitudes.shape
    virt = factors.shape[2]
    slots = min(RANKS * members, count)
    factors = factors[0]
    held_rows = factors.shape[0] // members
    chunk = held_rows // chunks

    def over_pair(value, distance):
        if distance == 0:
            return value
        return lax.ppermute(value, "pair", [(i, i ^ distance) for i in range(pairs)])

    def over_aux(value, distance):
        return lax.ppermute(value, "aux", [(i, i ^ distance) for i in range(shares)])

    def over_both(value, far, near):
        if (far, near) == (0, 0):
            return value
        route = [
            (i * shares + k, (i ^ far) * shares + (k ^ near))
            for i in range(pairs)
            for k in range(shares)
        ]
        return lax.ppermute(value, ("pair", "aux"), route)

    def trade(values, stride):
        if small:
            return jnp.stack([over_pair(values[i], i * stride) for i in range(pairs // stride)])
        order = lax.iota(jnp.int32, pairs // stride) ^ (me // stride)
        teams = [list(range(s, pairs, stride)) for s in range(stride)]
        got = lax.all_to_all(values[order], "pair", 0, 0, axis_index_groups=teams, tiled=True)
        return got[order]

    packed, positions = pack(place, block_list, owner_map, amplitudes, slots, bits, groups)
    if small:
        mine = jnp.stack([over_pair(packed[d >> bits], d) for d in range(pairs)])
    else:
        mine = trade(jnp.repeat(packed, members, axis=0), 1)
    rows = width // 2
    meta = mine[:, slots * rows : (slots + 0) * rows + slots, :3].astype(jnp.int32) - 1
    meta = meta.reshape(pairs * slots, 3)
    where = jnp.stack([meta[:, 0], (meta[:, 2] ^ local) * virt + meta[:, 1]])
    blocks = unpack(where, mine, slots)

    held = []
    for j in range(chunks):
        got = []
        for d in range(members):
            start = (local ^ d) * held_rows + j * chunk
            got.append(over_pair(lax.dynamic_slice_in_dim(factors, start, chunk, 0), d))
        got = jnp.stack(got)
        both = jnp.stack([got, over_aux(got, 1)], axis=1)
        both = jnp.transpose(both, (0, 3, 1, 2, 4))
        held.append(both.reshape(members * virt, 2 * chunk, depth))

    total = None
    for j in range(chunks):
        own, sent = contract(where, blocks, held[j], virt)
        got = over_pair(sent, members)
        stride = members * 2
        while stride < pairs:
            own = own + got.astype(jnp.float32)
            got = over_pair(own.astype(jnp.bfloat16), stride)
            stride *= 2
        total = project(where, own, got, held[j], total)

    quarter = rows // wide
    total = total.reshape(pairs // 2, 2, slots, wide, quarter, depth)
    summed = None
    for h in range(wide):
        piece = lax.dynamic_index_in_dim(total, part ^ h, 3, False)
        for y in range(2):
            value = piece[:, y]
            if (y, h) != (0, 0):
                value = over_both(value.astype(jnp.bfloat16), y, 2 * h).astype(jnp.float32)
            summed = value if summed is None else summed + value
    home = trade(summed.astype(jnp.bfloat16), 2).astype(jnp.float32)
    home = home.reshape(groups, members // 2, slots, quarter, depth)
    home = jnp.sum(home, axis=1).reshape(groups * slots, quarter, depth)
    result = home[positions].astype(jnp.bfloat16)
    pieces = jnp.stack([result] + [over_aux(result, a) for a in range(1, shares)])
    order = lax.iota(jnp.int32, shares)
    order = ((order % wide) * 2 + order // wide) ^ share
    return jnp.transpose(pieces[order], (1, 0, 2, 3)).reshape(count, width, depth)


def solution(mesh):
    placed = (P("pair", "aux", None, None), P("pair", None, None), P("pair", None), P())
    return jax.shard_map(
        on_device, mesh=mesh, in_specs=placed, out_specs=P("pair", None, None), check_vma=False
    )
```

```python
import jax
import jax.numpy as jnp
from jax import lax
from jax.experimental import pallas as pl
from jax.experimental.pallas import tpu as pltpu
from jax.sharding import PartitionSpec as P

CAP = 2
BATCH = 8
META = 16
MEMBERS = 4
FULL = 2
VMEM_BYTES = 48 * 1024 * 1024

SMEM_SPEC = pl.BlockSpec(memory_space=pltpu.SMEM)
VMEM_SPEC = pl.BlockSpec(memory_space=pltpu.VMEM)
PARAMS = pltpu.CompilerParams(vmem_limit_bytes=VMEM_BYTES)
COSTS = dict(pack=0, plan=10**13, contract=10**13, whole=0, project=0)


def cost(name):
    return pl.CostEstimate(flops=COSTS[name], bytes_accessed=0, transcendentals=0)


def pack_kernel(place_ref, list_ref, owner_ref, blocks_ref, out_ref):
    half = place_ref[1]
    count, width, depth = blocks_ref.shape
    rows = width // 2
    line = lax.broadcasted_iota(jnp.int32, (META, depth), 0)
    lane = lax.broadcasted_iota(jnp.int32, (META, depth), 1)
    meta = jnp.zeros((META, depth), jnp.float32)
    taken = pl.ds(pl.multiple_of(half * rows, rows), rows)
    for j in range(count):
        out_ref[j * rows : (j + 1) * rows, :] = blocks_ref[j, taken, :]
        owner = owner_ref[list_ref[j, 0]]
        for k, value in enumerate((list_ref[j, 1], list_ref[j, 2], owner)):
            meta = jnp.where((line == j) & (lane == k), value.astype(jnp.float32), meta)
    out_ref[pl.ds(count * rows, META), :] = meta.astype(out_ref.dtype)


def pack(place, block_list, owner_map, blocks):
    count, width, depth = blocks.shape
    return pl.pallas_call(
        pack_kernel,
        out_shape=jax.ShapeDtypeStruct((count * (width // 2) + META, depth), blocks.dtype),
        in_specs=[SMEM_SPEC, SMEM_SPEC, SMEM_SPEC, VMEM_SPEC],
        out_specs=VMEM_SPEC,
        compiler_params=PARAMS,
        cost_estimate=cost("pack"),
        name="pack",
    )(place, block_list, owner_map, blocks)


def plan_kernel(slots, owners, virt, meta_ref, out_ref):
    total = meta_ref.shape[0]
    room = total + BATCH

    def one(s, filled):
        owner = meta_ref[s, 2]
        sender = lax.div(s, slots)
        at = filled[0]
        for m in range(1, owners):
            at = jnp.where(owner == m, filled[m] + m * room, at)
        out_ref[0, at] = sender
        out_ref[1, at] = s - sender * slots
        out_ref[2, at] = meta_ref[s, 0]
        out_ref[3, at] = meta_ref[s, 1]
        out_ref[4, at] = s
        return tuple(n + (owner == m).astype(jnp.int32) for m, n in enumerate(filled))

    filled = lax.fori_loop(0, total, one, (jnp.int32(0),) * owners)
    for m, n in enumerate(filled):
        for u in range(BATCH):
            for k, value in enumerate((0, 0, virt, 0, total)):
                out_ref[k, m * room + n + u] = jnp.int32(value)
        out_ref[5, m] = lax.div(n + BATCH - 1, BATCH)


def plan(meta, slots, owners, virt):
    room = meta.shape[0] + BATCH
    return pl.pallas_call(
        lambda *refs: plan_kernel(slots, owners, virt, *refs),
        out_shape=jax.ShapeDtypeStruct((6, owners * room), jnp.int32),
        in_specs=[SMEM_SPEC],
        out_specs=SMEM_SPEC,
        cost_estimate=cost("plan"),
        name="plan",
    )(meta)


def over_slots(plan_ref, owners, picks, step):
    room = plan_ref.shape[1] // owners
    for owner, ref in picks:

        def batch(b, carry, owner=owner, ref=ref):
            step(ref, owner * room + b * BATCH)
            return carry

        lax.fori_loop(0, plan_ref[5, owner], batch, 0)


def add_blocks(plan_ref, blocks_ref, rows, sum_ref):
    def step(factors_ref, first):
        terms = []
        for i in range(BATCH):
            start = pl.multiple_of(plan_ref[1, first + i] * rows, rows)
            terms.append(
                lax.dot_general(
                    blocks_ref[plan_ref[0, first + i], pl.ds(start, rows), :],
                    factors_ref[plan_ref[3, first + i]],
                    (((1,), (1,)), ((), ())),
                    preferred_element_type=jnp.float32,
                )
            )
        for i in range(BATCH):
            sum_ref[plan_ref[2, first + i]] += terms[i]

    return step


def add_products(plan_ref, inter_ref, out_ref):
    def step(factors_ref, first):
        terms = []
        for i in range(BATCH):
            terms.append(
                jnp.dot(
                    inter_ref[plan_ref[2, first + i]],
                    factors_ref[plan_ref[3, first + i]],
                    preferred_element_type=jnp.float32,
                )
            )
        for i in range(BATCH):
            out_ref[plan_ref[4, first + i]] += terms[i]

    return step


def contract_kernel(owners, rows, place_ref, plan_ref, blocks_ref, *refs):
    own_ref, sent_ref = refs[-2:]
    own_ref[...] = jnp.zeros_like(own_ref)
    picks = [(place_ref[0] ^ d, ref) for d, ref in enumerate(refs[:-2])]
    over_slots(plan_ref, owners, picks, add_blocks(plan_ref, blocks_ref, rows, own_ref))
    sent_ref[...] = own_ref[pl.ds(0, sent_ref.shape[0])].astype(sent_ref.dtype)


def contract(place, listed, blocks, factors, owners, virt, rows):
    chunk = factors[0].shape[1]
    return pl.pallas_call(
        lambda *refs: contract_kernel(owners, rows, *refs),
        out_shape=(
            jax.ShapeDtypeStruct((virt + 1, rows, chunk), jnp.float32),
            jax.ShapeDtypeStruct((virt, rows, chunk), jnp.bfloat16),
        ),
        in_specs=[SMEM_SPEC] * 2 + [VMEM_SPEC] * (1 + len(factors)),
        out_specs=(VMEM_SPEC, VMEM_SPEC),
        compiler_params=PARAMS,
        cost_estimate=cost("contract"),
        name="contract",
    )(place, listed, blocks, *factors)


def whole_kernel(owners, rows, virt, plan_ref, blocks_ref, *refs):
    out_ref, sum_ref, inter_ref = refs[-3:]
    factors_ref = refs[0]
    so_far = refs[1:-3]
    out_ref[...] = so_far[0][...] if so_far else jnp.zeros_like(out_ref)
    sum_ref[...] = jnp.zeros_like(sum_ref)
    picks = [(k, factors_ref.at[pl.ds(k * virt, virt)]) for k in range(owners)]
    over_slots(plan_ref, owners, picks, add_blocks(plan_ref, blocks_ref, rows, sum_ref))
    inter_ref[...] = sum_ref[...].astype(inter_ref.dtype)
    over_slots(plan_ref, owners, picks, add_products(plan_ref, inter_ref, out_ref))


def whole(listed, blocks, factors, so_far, owners, virt, rows, total):
    chunk, depth = factors.shape[1:]
    so_far = [] if so_far is None else [so_far]
    return pl.pallas_call(
        lambda *refs: whole_kernel(owners, rows, virt, *refs),
        out_shape=jax.ShapeDtypeStruct((total + 1, rows, depth), jnp.float32),
        in_specs=[SMEM_SPEC] + [VMEM_SPEC] * (2 + len(so_far)),
        out_specs=VMEM_SPEC,
        scratch_shapes=[
            pltpu.VMEM((virt + 1, rows, chunk), jnp.float32),
            pltpu.VMEM((virt + 1, rows, chunk), jnp.bfloat16),
        ],
        compiler_params=PARAMS,
        cost_estimate=cost("whole"),
        name="whole",
    )(listed, blocks, factors, *so_far)


def project_kernel(owners, members, place_ref, plan_ref, own_ref, got_ref, so_far_ref, *refs):
    out_ref, inter_ref = refs[-2:]
    virt = got_ref.shape[0]
    summed = own_ref[pl.ds(0, virt)] + got_ref[...].astype(jnp.float32)
    inter_ref[pl.ds(0, virt)] = summed.astype(inter_ref.dtype)
    inter_ref[virt] = jnp.zeros(inter_ref.shape[1:], inter_ref.dtype)
    out_ref[...] = so_far_ref[...]
    picks = [(place_ref[0] ^ d, ref) for d, ref in enumerate(refs[:members])]
    over_slots(plan_ref, owners, picks, add_products(plan_ref, inter_ref, out_ref))


def project(place, listed, own, got, factors, so_far, owners):
    return pl.pallas_call(
        lambda *refs: project_kernel(owners, len(factors), *refs),
        out_shape=jax.ShapeDtypeStruct(so_far.shape, jnp.float32),
        in_specs=[SMEM_SPEC] * 2 + [VMEM_SPEC] * (3 + len(factors)),
        out_specs=VMEM_SPEC,
        scratch_shapes=[pltpu.VMEM(own.shape, jnp.bfloat16)],
        compiler_params=PARAMS,
        cost_estimate=cost("project"),
        name="project",
    )(place, listed, own, got, so_far, *factors)


def after(value, *others):
    return lax.optimization_barrier((value, *others))[0]


def near_plan(factors, amplitudes, block_list, owner_map):
    pairs = lax.axis_size("pair")
    shares = lax.axis_size("aux")
    wide = shares // 2
    me = lax.axis_index("pair")
    share = lax.axis_index("aux")
    half, part = share & 1, share >> 1
    place = jnp.stack([me, half]).astype(jnp.int32)
    slots, width, depth = amplitudes.shape
    rows = width // 2
    total = pairs * slots
    virt = factors.shape[2]
    factors = factors[0]
    full_rows = factors.shape[0] // FULL
    full_chunk = full_rows // pairs
    chunk = (factors.shape[0] - full_rows) // MEMBERS

    def over_pair(value, distance):
        if distance == 0:
            return value
        return lax.ppermute(value, "pair", [(i, i ^ distance) for i in range(pairs)])

    def over_aux(value, distance):
        return lax.ppermute(value, "aux", [(i, i ^ distance) for i in range(shares)])

    def over_both(value, far, near):
        route = [
            (i * shares + k, (i ^ far) * shares + (k ^ near))
            for i in range(pairs)
            for k in range(shares)
        ]
        return lax.ppermute(value, ("pair", "aux"), route)

    full = factors[:full_rows].reshape(pairs, full_chunk, virt, depth)
    full, turn = lax.optimization_barrier((full, me))
    starts = [full_rows + ((turn & (MEMBERS - 1)) ^ d) * chunk for d in range(MEMBERS)]
    pieces = [lax.dynamic_slice_in_dim(factors, start, chunk, 0) for start in starts]
    pieces = [jnp.transpose(piece, (1, 0, 2)) for piece in pieces]
    full = lax.all_to_all(full, "pair", 0, 0, tiled=True)

    packed = pack(place, block_list, owner_map, after(amplitudes, turn))
    near = jnp.stack([over_pair(packed, 2 * i) for i in range(pairs // 2)])
    blocks = jnp.concatenate([near, over_pair(near, 1)])
    meta = blocks[:, slots * rows : slots * rows + slots, :3].astype(jnp.int32)
    listed = plan(meta.reshape(total, 3), slots, pairs, virt)

    mine = [pieces[0]]
    for d in range(1, MEMBERS):
        mine.append(after(over_pair(pieces[d], d), blocks))
    other = [over_aux(piece, 1) for piece in mine]
    work = []
    for held in (mine, other):
        own, sent = contract(place, listed, blocks, held, pairs, virt, rows)
        work.append((own, over_pair(sent, MEMBERS), held))
    full = jnp.transpose(after(full, sent), (0, 2, 1, 3)).reshape(pairs * virt, full_chunk, depth)
    out = None
    for held in (full, over_aux(full, 1)):
        out = whole(listed, blocks, held, out, pairs, virt, rows, total)
    for own, got, held in work:
        out = project(place, listed, own, got, held, out, pairs)

    quarter = rows // wide
    out = out[:total].reshape(2, pairs // 2, slots, wide, quarter, depth)
    summed = None
    for h in range(wide):
        piece = lax.dynamic_index_in_dim(out, part ^ h, 3, False)
        for y in range(2):
            value = piece[y]
            if (y, h) != (0, 0):
                value = over_both(value.astype(jnp.bfloat16), y, 2 * h).astype(jnp.float32)
            summed = value if summed is None else summed + value
    summed = summed.astype(jnp.bfloat16)
    home = None
    for i in range(pairs // 2):
        value = over_pair(summed[i], 2 * i).astype(jnp.float32)
        home = value if home is None else home + value
    result = home.astype(jnp.bfloat16)
    quarters = jnp.stack([result] + [over_aux(result, a) for a in range(1, shares)])
    order = lax.iota(jnp.int32, shares)
    order = ((order % wide) * 2 + order // wide) ^ share
    return jnp.transpose(quarters[order], (1, 0, 2, 3)).reshape(slots, width, depth)


def far_plan(factors, amplitudes, block_list, owner_map):
    pair_count = lax.axis_size("pair")
    slot_total = pair_count * CAP
    block_count = amplitudes.shape[0]
    block_width = amplitudes.shape[1]
    virt_blocks = factors.shape[2]
    share_rows = factors.shape[1]
    orbital_total = owner_map.shape[0]
    orbitals = block_list[:, 0]
    block_a = block_list[:, 1]
    block_c = block_list[:, 2]
    matches = orbitals[:, None] == lax.iota(jnp.int32, orbital_total)[None, :]
    owners = jnp.sum(jnp.where(matches, owner_map[None, :], 0), axis=1)
    owner_hits = (owners[:, None] == lax.iota(jnp.int32, pair_count)[None, :]).astype(jnp.int32)
    earlier = jnp.cumsum(owner_hits, axis=0) - owner_hits
    slot_rank = jnp.sum(earlier * owner_hits, axis=1)
    slots = owners * CAP + slot_rank
    placing = slots[:, None] == lax.iota(jnp.int32, slot_total)[None, :]
    place_matrix = placing.astype(jnp.bfloat16)
    flat_blocks = amplitudes.reshape(block_count, block_width * block_width)
    send_blocks = jnp.einsum(
        "js,jm->sm", place_matrix, flat_blocks, preferred_element_type=jnp.float32
    )
    send_blocks = send_blocks.astype(jnp.bfloat16).reshape(
        pair_count, CAP, block_width, block_width
    )
    send_a = jnp.sum(jnp.where(placing, block_a[:, None] + 1, 0), axis=0)
    send_c = jnp.sum(jnp.where(placing, block_c[:, None] + 1, 0), axis=0)
    send_index = (
        jnp.stack([send_a, send_c], axis=-1).astype(jnp.bfloat16).reshape(pair_count, CAP, 2)
    )
    recv_blocks, recv_index = (
        lax.all_to_all(send_blocks, "pair", split_axis=0, concat_axis=0, tiled=True),
        lax.all_to_all(send_index, "pair", split_axis=0, concat_axis=0, tiled=True),
    )
    recv_index = recv_index.reshape(slot_total, 2).astype(jnp.int32) - 1
    slot_a = recv_index[:, 0]
    slot_c = recv_index[:, 1]
    onehot_a = (slot_a[:, None] == lax.iota(jnp.int32, virt_blocks)[None, :]).astype(jnp.bfloat16)
    onehot_c = (slot_c[:, None] == lax.iota(jnp.int32, virt_blocks)[None, :]).astype(jnp.bfloat16)
    combined = (onehot_c[:, :, None] * onehot_a[:, None, :]).reshape(
        slot_total, virt_blocks * virt_blocks
    )
    recv_flat = recv_blocks.reshape(slot_total, block_width * block_width)
    weights = jnp.einsum("sm,sn->mn", combined, recv_flat, preferred_element_type=jnp.float32)
    weights = weights.reshape(virt_blocks, virt_blocks, block_width, block_width)
    weights = jnp.transpose(weights, (0, 3, 1, 2)).reshape(
        virt_blocks * block_width, virt_blocks * block_width
    )
    weights = weights.astype(jnp.bfloat16)
    factor_flat = factors.reshape(share_rows, virt_blocks * block_width)
    factor_rows = factor_flat
    inter_share = lax.psum_scatter(
        jnp.dot(factor_rows, weights, preferred_element_type=jnp.float32),
        "pair",
        scatter_dimension=0,
        tiled=True,
    )
    inter_share = inter_share.astype(jnp.bfloat16)
    shard_rows = lax.all_gather(inter_share, "pair", axis=0, tiled=True)
    height = shard_rows.shape[0]
    factor_rows = factor_flat
    left = shard_rows.reshape(height, virt_blocks, block_width)
    right = factor_rows.reshape(height, virt_blocks, block_width)
    projected = jnp.einsum("qAa,qCc->ACac", left, right, preferred_element_type=jnp.float32)
    safe_a = jnp.maximum(slot_a, 0)
    safe_c = jnp.maximum(slot_c, 0)
    summed = lax.psum(projected, "aux")
    picked = summed[safe_a, safe_c].astype(jnp.bfloat16)
    picked = picked.reshape(pair_count, CAP, block_width, block_width)
    returned = lax.all_to_all(picked, "pair", split_axis=0, concat_axis=0, tiled=True)
    returned = returned.reshape(slot_total, block_width * block_width)
    result = jnp.einsum("js,sm->jm", place_matrix, returned, preferred_element_type=jnp.float32)
    return result.astype(jnp.bfloat16).reshape(block_count, block_width, block_width)


def solution(mesh):
    placed = (P("pair", "aux", None, None), P("pair", None, None), P("pair", None), P())
    on_device = near_plan if mesh.shape["pair"] == 2 * MEMBERS else far_plan
    return jax.shard_map(
        on_device, mesh=mesh, in_specs=placed, out_specs=P("pair", None, None), check_vma=False
    )
```

```python
import jax
import jax.numpy as jnp
from jax import lax
from jax.experimental import pallas as pl
from jax.experimental.pallas import tpu as pltpu
from jax.sharding import PartitionSpec as P

CAP = 2
BATCH = 8
META = 16
MEMBERS = 4
FULL = 2
VMEM_BYTES = 16 * 1024 * 1024

SMEM_SPEC = pl.BlockSpec(memory_space=pltpu.SMEM)
VMEM_SPEC = pl.BlockSpec(memory_space=pltpu.VMEM)
PARAMS = pltpu.CompilerParams(vmem_limit_bytes=VMEM_BYTES)
COSTS = dict(pack=0, plan=10**13, contract=10**13, whole=0, project=0)


def cost(name):
    return pl.CostEstimate(flops=COSTS[name], bytes_accessed=0, transcendentals=0)


def pack_kernel(place_ref, list_ref, owner_ref, blocks_ref, out_ref):
    half = place_ref[1]
    count, width, depth = blocks_ref.shape
    rows = width // 2
    line = lax.broadcasted_iota(jnp.int32, (META, depth), 0)
    lane = lax.broadcasted_iota(jnp.int32, (META, depth), 1)
    meta = jnp.zeros((META, depth), jnp.float32)
    taken = pl.ds(pl.multiple_of(half * rows, rows), rows)
    for j in range(count):
        out_ref[j * rows : (j + 1) * rows, :] = blocks_ref[j, taken, :]
        owner = owner_ref[list_ref[j, 0]]
        for k, value in enumerate((list_ref[j, 1], list_ref[j, 2], owner)):
            meta = jnp.where((line == j) & (lane == k), value.astype(jnp.float32), meta)
    out_ref[pl.ds(count * rows, META), :] = meta.astype(out_ref.dtype)


def pack(place, block_list, owner_map, blocks):
    count, width, depth = blocks.shape
    return pl.pallas_call(
        pack_kernel,
        out_shape=jax.ShapeDtypeStruct((count * (width // 2) + META, depth), blocks.dtype),
        in_specs=[SMEM_SPEC, SMEM_SPEC, SMEM_SPEC, VMEM_SPEC],
        out_specs=VMEM_SPEC,
        compiler_params=PARAMS,
        cost_estimate=cost("pack"),
        name="pack",
    )(place, block_list, owner_map, blocks)


def plan_kernel(slots, owners, virt, meta_ref, out_ref, filled_ref):
    total = meta_ref.shape[0]
    room = total + BATCH
    for m in range(owners):
        filled_ref[m] = m * room

    def one(s, place):
        owner = meta_ref[s, 2]
        sender, first = place
        where = meta_ref[s, 0] * 16 + meta_ref[s, 1]
        at = filled_ref[owner]
        out_ref[at] = ((s * 16 + sender) * 16 + s - first) * 256 + where
        filled_ref[owner] = at + 1
        over = s + 1 - first == slots
        return sender + over.astype(jnp.int32), jnp.where(over, s + 1, first)

    lax.fori_loop(0, total, one, (jnp.int32(0), jnp.int32(0)))
    for m in range(owners):
        n = filled_ref[m]
        for u in range(BATCH):
            out_ref[n + u] = jnp.int32(total * 65536 + virt * 16)
        out_ref[owners * room + m] = lax.div(n - m * room + BATCH - 1, BATCH)


def plan(meta, slots, owners, virt):
    room = meta.shape[0] + BATCH
    return pl.pallas_call(
        lambda *refs: plan_kernel(slots, owners, virt, *refs),
        out_shape=jax.ShapeDtypeStruct((owners * room + owners,), jnp.int32),
        in_specs=[SMEM_SPEC],
        out_specs=SMEM_SPEC,
        scratch_shapes=[pltpu.SMEM((owners,), jnp.int32)],
        cost_estimate=cost("plan"),
        name="plan",
    )(meta)


def over_slots(plan_ref, owners, picks, step):
    room = plan_ref.shape[0] // owners - 1
    for owner, ref in picks:

        def batch(b, carry, owner=owner, ref=ref):
            step(ref, owner * room + b * BATCH)
            return carry

        lax.fori_loop(0, plan_ref[owners * room + owner], batch, 0)


def add_blocks(plan_ref, blocks_ref, rows, sum_ref):
    def step(factors_ref, first):
        words = [plan_ref[first + i] for i in range(BATCH)]
        terms = []
        for word in words:
            start = pl.multiple_of(((word >> 8) & 15) * rows, rows)
            terms.append(
                lax.dot_general(
                    blocks_ref[(word >> 12) & 15, pl.ds(start, rows), :],
                    factors_ref[word & 15],
                    (((1,), (1,)), ((), ())),
                    preferred_element_type=jnp.float32,
                )
            )
        for word, term in zip(words, terms):
            sum_ref[(word >> 4) & 15] += term

    return step


def add_products(plan_ref, inter_ref, out_ref):
    def step(factors_ref, first):
        words = [plan_ref[first + i] for i in range(BATCH)]
        terms = []
        for word in words:
            terms.append(
                jnp.dot(
                    inter_ref[(word >> 4) & 15],
                    factors_ref[word & 15],
                    preferred_element_type=jnp.float32,
                )
            )
        for word, term in zip(words, terms):
            out_ref[word >> 16] += term

    return step


def contract_kernel(owners, rows, place_ref, plan_ref, blocks_ref, others_ref, *refs):
    pieces = refs[:MEMBERS]
    own_ref, same_ref, cross_ref, stack_ref, sum_ref, sems = refs[MEMBERS:]
    virt = own_ref.shape[0]
    copies = [
        pltpu.make_async_copy(ref, stack_ref.at[pl.ds(d * virt, virt)], sems.at[d])
        for d, ref in enumerate(pieces)
    ]
    for copy in copies:
        copy.start()
    sum_ref[...] = jnp.zeros_like(sum_ref)

    def step(factors_ref, first):
        words = [plan_ref[first + i] for i in range(BATCH)]
        terms = []
        for word in words:
            start = pl.multiple_of(((word >> 8) & 15) * rows, rows)
            halves = [ref[(word >> 12) & 15, pl.ds(start, rows), :] for ref in (blocks_ref, others_ref)]
            terms.append(
                lax.dot_general(
                    jnp.concatenate(halves),
                    factors_ref[word & 15],
                    (((1,), (1,)), ((), ())),
                    preferred_element_type=jnp.float32,
                )
            )
        for word, term in zip(words, terms):
            sum_ref[(word >> 4) & 15] += term

    picks = [(place_ref[0] ^ d, ref) for d, ref in enumerate(pieces)]
    over_slots(plan_ref, owners, picks, step)
    own = sum_ref[pl.ds(0, virt), pl.ds(0, rows), :]
    own_ref[...] = own
    same_ref[...] = own.astype(same_ref.dtype)
    cross_ref[...] = sum_ref[pl.ds(0, virt), pl.ds(rows, rows), :].astype(cross_ref.dtype)
    for copy in copies:
        copy.wait()


def contract(place, listed, blocks, others, factors, owners, virt, rows):
    chunk, depth = factors[0].shape[1:]
    sent = jax.ShapeDtypeStruct((virt, rows, chunk), jnp.bfloat16)
    stack = jax.ShapeDtypeStruct((MEMBERS * virt, chunk, depth), jnp.bfloat16)
    return pl.pallas_call(
        lambda *refs: contract_kernel(owners, rows, *refs),
        out_shape=(jax.ShapeDtypeStruct((virt, rows, chunk), jnp.float32), sent, sent, stack),
        in_specs=[SMEM_SPEC] * 2 + [VMEM_SPEC] * (2 + len(factors)),
        out_specs=(VMEM_SPEC,) * 3 + (pl.BlockSpec(memory_space=pl.ANY),),
        scratch_shapes=[
            pltpu.VMEM((virt + 1, 2 * rows, chunk), jnp.float32),
            pltpu.SemaphoreType.DMA((MEMBERS,)),
        ],
        compiler_params=PARAMS,
        cost_estimate=cost("contract"),
        name="contract",
    )(place, listed, blocks, others, *factors)


def whole_kernel(owners, rows, virt, plan_ref, blocks_ref, *refs):
    out_ref, sum_ref, inter_ref = refs[-3:]
    factors_ref = refs[0]
    so_far = refs[1:-3]
    out_ref[...] = so_far[0][...] if so_far else jnp.zeros_like(out_ref)
    sum_ref[...] = jnp.zeros_like(sum_ref)
    picks = [(k, factors_ref.at[pl.ds(k * virt, virt)]) for k in range(owners)]
    over_slots(plan_ref, owners, picks, add_blocks(plan_ref, blocks_ref, rows, sum_ref))
    inter_ref[...] = sum_ref[...].astype(inter_ref.dtype)
    over_slots(plan_ref, owners, picks, add_products(plan_ref, inter_ref, out_ref))


def whole(listed, blocks, factors, so_far, owners, virt, rows, total):
    chunk, depth = factors.shape[1:]
    so_far = [] if so_far is None else [so_far]
    return pl.pallas_call(
        lambda *refs: whole_kernel(owners, rows, virt, *refs),
        out_shape=jax.ShapeDtypeStruct((total + 1, rows, depth), jnp.float32),
        in_specs=[SMEM_SPEC] + [VMEM_SPEC] * (2 + len(so_far)),
        out_specs=VMEM_SPEC,
        scratch_shapes=[
            pltpu.VMEM((virt + 1, rows, chunk), jnp.float32),
            pltpu.VMEM((virt + 1, rows, chunk), jnp.bfloat16),
        ],
        compiler_params=PARAMS,
        cost_estimate=cost("whole"),
        name="whole",
    )(listed, blocks, factors, *so_far)


def project_kernel(owners, place_ref, plan_ref, own_ref, got_ref, so_far_ref, *refs):
    out_ref, inter_ref = refs[-2:]
    virt = got_ref.shape[0]
    summed = own_ref[...].astype(jnp.float32) + got_ref[...].astype(jnp.float32)
    inter_ref[pl.ds(0, virt)] = summed.astype(inter_ref.dtype)
    inter_ref[virt] = jnp.zeros(inter_ref.shape[1:], inter_ref.dtype)
    out_ref[...] = so_far_ref[...]
    pieces = refs[:-2]
    if len(pieces) == 1:
        pieces = [refs[0].at[pl.ds(d * virt, virt)] for d in range(MEMBERS)]
    picks = [(place_ref[0] ^ d, ref) for d, ref in enumerate(pieces)]
    over_slots(plan_ref, owners, picks, add_products(plan_ref, inter_ref, out_ref))


def project(place, listed, own, got, factors, so_far, owners):
    virt, rows, chunk = got.shape
    return pl.pallas_call(
        lambda *refs: project_kernel(owners, *refs),
        out_shape=jax.ShapeDtypeStruct(so_far.shape, jnp.float32),
        in_specs=[SMEM_SPEC] * 2 + [VMEM_SPEC] * (3 + len(factors)),
        out_specs=VMEM_SPEC,
        scratch_shapes=[pltpu.VMEM((virt + 1, rows, chunk), jnp.bfloat16)],
        compiler_params=PARAMS,
        cost_estimate=cost("project"),
        name="project",
    )(place, listed, own, got, so_far, *factors)


def touch(values, *others):
    values = list(values)
    anywhere = pl.BlockSpec(memory_space=pl.ANY)
    return pl.pallas_call(
        lambda *refs: None,
        out_shape=[jax.ShapeDtypeStruct(value.shape, value.dtype) for value in values],
        in_specs=[anywhere] * (len(values) + len(others)),
        out_specs=[anywhere] * len(values),
        input_output_aliases={i: i for i in range(len(values))},
        name="touch",
    )(*values, *others)


def after(value, *others):
    return lax.optimization_barrier((value, *others))[0]


def near_plan(factors, amplitudes, block_list, owner_map):
    pairs = lax.axis_size("pair")
    shares = lax.axis_size("aux")
    wide = shares // 2
    me = lax.axis_index("pair")
    share = lax.axis_index("aux")
    half, part = share & 1, share >> 1
    place = jnp.stack([me, half]).astype(jnp.int32)
    slots, width, depth = amplitudes.shape
    rows = width // 2
    total = pairs * slots
    virt = factors.shape[2]
    factors = factors[0]
    full_rows = factors.shape[0] // FULL
    full_chunk = full_rows // pairs
    chunk = (factors.shape[0] - full_rows) // MEMBERS

    def over_pair(value, distance):
        if distance == 0:
            return value
        return lax.ppermute(value, "pair", [(i, i ^ distance) for i in range(pairs)])

    def over_aux(value, distance):
        return lax.ppermute(value, "aux", [(i, i ^ distance) for i in range(shares)])

    def over_both(value, far, near):
        route = [
            (i * shares + k, (i ^ far) * shares + (k ^ near))
            for i in range(pairs)
            for k in range(shares)
        ]
        return lax.ppermute(value, ("pair", "aux"), route)

    full = factors[:full_rows].reshape(pairs, full_chunk, virt, depth)
    full, turn = lax.optimization_barrier((full, me))
    starts = [full_rows + ((turn & (MEMBERS - 1)) ^ d) * chunk for d in range(MEMBERS)]
    pieces = [lax.dynamic_slice_in_dim(factors, start, chunk, 0) for start in starts]
    pieces = [jnp.transpose(piece, (1, 0, 2)) for piece in pieces]

    packed = pack(place, block_list, owner_map, after(amplitudes, turn))
    near = jnp.stack([over_pair(packed, 2 * i) for i in range(pairs // 2)])
    blocks = jnp.concatenate([near, over_pair(near, 1)])
    meta = blocks[:, slots * rows : slots * rows + slots, :3].astype(jnp.int32)
    listed = plan(meta.reshape(total, 3), slots, pairs, virt)

    full = lax.all_to_all(after(full, near), "pair", 0, 0, tiled=True)
    for d in (1, 3):
        pieces[d] = after(pieces[d], near)

    others = over_aux(blocks, 1)
    mine = [over_pair(pieces[d], d) for d in range(1, MEMBERS)]
    mine = [pieces[0], *touch(mine, listed, others)]
    own, same, cross, stack = contract(place, listed, blocks, others, mine, pairs, virt, rows)
    got = over_pair(same, MEMBERS), over_both(cross, MEMBERS, 1)
    own = own, over_aux(cross, 1)
    work = list(zip(own, got, (mine, [over_aux(stack, 1)])))
    full = jnp.transpose(after(full, same), (0, 2, 1, 3)).reshape(pairs * virt, full_chunk, depth)
    out = None
    for held in (full, over_aux(full, 1)):
        out = whole(listed, blocks, held, out, pairs, virt, rows, total)
    for own, got, held in work:
        out = project(place, listed, own, got, held, out, pairs)

    quarter = rows // wide
    out = out[:total].reshape(2, pairs // 2, slots, wide, quarter, depth)
    summed = None
    for h in range(wide):
        piece = lax.dynamic_index_in_dim(out, part ^ h, 3, False)
        for y in range(2):
            value = piece[y]
            if (y, h) != (0, 0):
                value = over_both(value.astype(jnp.bfloat16), y, 2 * h).astype(jnp.float32)
            summed = value if summed is None else summed + value
    summed = summed.astype(jnp.bfloat16)
    home = None
    for i in range(pairs // 2):
        value = over_pair(summed[i], 2 * i).astype(jnp.float32)
        home = value if home is None else home + value
    result = home.astype(jnp.bfloat16)
    quarters = jnp.stack([result] + [over_aux(result, a) for a in range(1, shares)])
    order = lax.iota(jnp.int32, shares)
    order = ((order % wide) * 2 + order // wide) ^ share
    return jnp.transpose(quarters[order], (1, 0, 2, 3)).reshape(slots, width, depth)


def far_plan(factors, amplitudes, block_list, owner_map):
    pair_count = lax.axis_size("pair")
    slot_total = pair_count * CAP
    block_count = amplitudes.shape[0]
    block_width = amplitudes.shape[1]
    virt_blocks = factors.shape[2]
    share_rows = factors.shape[1]
    orbital_total = owner_map.shape[0]
    orbitals = block_list[:, 0]
    block_a = block_list[:, 1]
    block_c = block_list[:, 2]
    matches = orbitals[:, None] == lax.iota(jnp.int32, orbital_total)[None, :]
    owners = jnp.sum(jnp.where(matches, owner_map[None, :], 0), axis=1)
    owner_hits = (owners[:, None] == lax.iota(jnp.int32, pair_count)[None, :]).astype(jnp.int32)
    earlier = jnp.cumsum(owner_hits, axis=0) - owner_hits
    slot_rank = jnp.sum(earlier * owner_hits, axis=1)
    slots = owners * CAP + slot_rank
    placing = slots[:, None] == lax.iota(jnp.int32, slot_total)[None, :]
    place_matrix = placing.astype(jnp.bfloat16)
    flat_blocks = amplitudes.reshape(block_count, block_width * block_width)
    send_blocks = jnp.einsum(
        "js,jm->sm", place_matrix, flat_blocks, preferred_element_type=jnp.float32
    )
    send_blocks = send_blocks.astype(jnp.bfloat16).reshape(
        pair_count, CAP, block_width, block_width
    )
    send_a = jnp.sum(jnp.where(placing, block_a[:, None] + 1, 0), axis=0)
    send_c = jnp.sum(jnp.where(placing, block_c[:, None] + 1, 0), axis=0)
    send_index = (
        jnp.stack([send_a, send_c], axis=-1).astype(jnp.bfloat16).reshape(pair_count, CAP, 2)
    )
    recv_blocks, recv_index = (
        lax.all_to_all(send_blocks, "pair", split_axis=0, concat_axis=0, tiled=True),
        lax.all_to_all(send_index, "pair", split_axis=0, concat_axis=0, tiled=True),
    )
    recv_index = recv_index.reshape(slot_total, 2).astype(jnp.int32) - 1
    slot_a = recv_index[:, 0]
    slot_c = recv_index[:, 1]
    onehot_a = (slot_a[:, None] == lax.iota(jnp.int32, virt_blocks)[None, :]).astype(jnp.bfloat16)
    onehot_c = (slot_c[:, None] == lax.iota(jnp.int32, virt_blocks)[None, :]).astype(jnp.bfloat16)
    combined = (onehot_c[:, :, None] * onehot_a[:, None, :]).reshape(
        slot_total, virt_blocks * virt_blocks
    )
    recv_flat = recv_blocks.reshape(slot_total, block_width * block_width)
    weights = jnp.einsum("sm,sn->mn", combined, recv_flat, preferred_element_type=jnp.float32)
    weights = weights.reshape(virt_blocks, virt_blocks, block_width, block_width)
    weights = jnp.transpose(weights, (0, 3, 1, 2)).reshape(
        virt_blocks * block_width, virt_blocks * block_width
    )
    weights = weights.astype(jnp.bfloat16)
    factor_flat = factors.reshape(share_rows, virt_blocks * block_width)
    factor_rows = factor_flat
    inter_share = lax.psum_scatter(
        jnp.dot(factor_rows, weights, preferred_element_type=jnp.float32),
        "pair",
        scatter_dimension=0,
        tiled=True,
    )
    inter_share = inter_share.astype(jnp.bfloat16)
    shard_rows = lax.all_gather(inter_share, "pair", axis=0, tiled=True)
    height = shard_rows.shape[0]
    factor_rows = factor_flat
    left = shard_rows.reshape(height, virt_blocks, block_width)
    right = factor_rows.reshape(height, virt_blocks, block_width)
    projected = jnp.einsum("qAa,qCc->ACac", left, right, preferred_element_type=jnp.float32)
    safe_a = jnp.maximum(slot_a, 0)
    safe_c = jnp.maximum(slot_c, 0)
    summed = lax.psum(projected, "aux")
    picked = summed[safe_a, safe_c].astype(jnp.bfloat16)
    picked = picked.reshape(pair_count, CAP, block_width, block_width)
    returned = lax.all_to_all(picked, "pair", split_axis=0, concat_axis=0, tiled=True)
    returned = returned.reshape(slot_total, block_width * block_width)
    result = jnp.einsum("js,sm->jm", place_matrix, returned, preferred_element_type=jnp.float32)
    return result.astype(jnp.bfloat16).reshape(block_count, block_width, block_width)


def solution(mesh):
    placed = (P("pair", "aux", None, None), P("pair", None, None), P("pair", None), P())
    on_device = near_plan if mesh.shape["pair"] == 2 * MEMBERS else far_plan
    return jax.shard_map(
        on_device, mesh=mesh, in_specs=placed, out_specs=P("pair", None, None), check_vma=False
    )
```

```python
import jax
import jax.numpy as jnp
from jax import lax
from jax.experimental import pallas as pl
from jax.experimental.pallas import tpu as pltpu
from jax.sharding import PartitionSpec as P

CAP = 2
BATCH = 8
META = 16
MEMBERS = 4
FULL = 2
VMEM_BYTES = 16 * 1024 * 1024

SMEM_SPEC = pl.BlockSpec(memory_space=pltpu.SMEM)
VMEM_SPEC = pl.BlockSpec(memory_space=pltpu.VMEM)
PARAMS = pltpu.CompilerParams(vmem_limit_bytes=VMEM_BYTES)
COSTS = dict(pack=0, plan=10**13, contract=10**13, whole=0, project=0)


def cost(name):
    return pl.CostEstimate(flops=COSTS[name], bytes_accessed=0, transcendentals=0)


def pack_kernel(place_ref, list_ref, owner_ref, blocks_ref, out_ref):
    half = place_ref[1]
    count, width, depth = blocks_ref.shape
    rows = width // 2
    line = lax.broadcasted_iota(jnp.int32, (META, depth), 0)
    lane = lax.broadcasted_iota(jnp.int32, (META, depth), 1)
    meta = jnp.zeros((META, depth), jnp.float32)
    taken = pl.ds(pl.multiple_of(half * rows, rows), rows)
    for j in range(count):
        out_ref[j * rows : (j + 1) * rows, :] = blocks_ref[j, taken, :]
        owner = owner_ref[list_ref[j, 0]]
        for k, value in enumerate((list_ref[j, 1], list_ref[j, 2], owner)):
            meta = jnp.where((line == j) & (lane == k), value.astype(jnp.float32), meta)
    out_ref[pl.ds(count * rows, META), :] = meta.astype(out_ref.dtype)


def pack(place, block_list, owner_map, blocks):
    count, width, depth = blocks.shape
    return pl.pallas_call(
        pack_kernel,
        out_shape=jax.ShapeDtypeStruct((count * (width // 2) + META, depth), blocks.dtype),
        in_specs=[SMEM_SPEC, SMEM_SPEC, SMEM_SPEC, VMEM_SPEC],
        out_specs=VMEM_SPEC,
        compiler_params=PARAMS,
        cost_estimate=cost("pack"),
        name="pack",
    )(place, block_list, owner_map, blocks)


def plan_kernel(slots, owners, virt, meta_ref, out_ref, filled_ref):
    total = meta_ref.shape[0]
    room = total + BATCH
    for m in range(owners):
        filled_ref[m] = m * room

    def one(s, place):
        owner = meta_ref[s, 2]
        sender, first = place
        where = meta_ref[s, 0] * 16 + meta_ref[s, 1]
        at = filled_ref[owner]
        out_ref[at] = ((s * 16 + sender) * 16 + s - first) * 256 + where
        filled_ref[owner] = at + 1
        over = s + 1 - first == slots
        return sender + over.astype(jnp.int32), jnp.where(over, s + 1, first)

    lax.fori_loop(0, total, one, (jnp.int32(0), jnp.int32(0)))
    for m in range(owners):
        n = filled_ref[m]
        for u in range(BATCH):
            out_ref[n + u] = jnp.int32(total * 65536 + virt * 16)
        out_ref[owners * room + m] = lax.div(n - m * room + BATCH - 1, BATCH)


def plan(meta, slots, owners, virt):
    room = meta.shape[0] + BATCH
    return pl.pallas_call(
        lambda *refs: plan_kernel(slots, owners, virt, *refs),
        out_shape=jax.ShapeDtypeStruct((owners * room + owners,), jnp.int32),
        in_specs=[SMEM_SPEC],
        out_specs=SMEM_SPEC,
        scratch_shapes=[pltpu.SMEM((owners,), jnp.int32)],
        cost_estimate=cost("plan"),
        name="plan",
    )(meta)


def over_slots(plan_ref, owners, picks, step):
    room = plan_ref.shape[0] // owners - 1
    for owner, ref in picks:

        def batch(b, carry, owner=owner, ref=ref):
            step(ref, owner * room + b * BATCH)
            return carry

        lax.fori_loop(0, plan_ref[owners * room + owner], batch, 0)


def add_blocks(plan_ref, blocks_ref, rows, sum_ref):
    def step(factors_ref, first):
        words = [plan_ref[first + i] for i in range(BATCH)]
        terms = []
        for word in words:
            start = pl.multiple_of(((word >> 8) & 15) * rows, rows)
            terms.append(
                lax.dot_general(
                    blocks_ref[(word >> 12) & 15, pl.ds(start, rows), :],
                    factors_ref[word & 15],
                    (((1,), (1,)), ((), ())),
                    preferred_element_type=jnp.float32,
                )
            )
        for word, term in zip(words, terms):
            sum_ref[(word >> 4) & 15] += term

    return step


def add_products(plan_ref, inter_ref, out_ref):
    def step(factors_ref, first):
        words = [plan_ref[first + i] for i in range(BATCH)]
        terms = []
        for word in words:
            terms.append(
                jnp.dot(
                    inter_ref[(word >> 4) & 15],
                    factors_ref[word & 15],
                    preferred_element_type=jnp.float32,
                )
            )
        for word, term in zip(words, terms):
            out_ref[word >> 16] += term

    return step


def contract_kernel(owners, rows, place_ref, plan_ref, blocks_ref, others_ref, *refs):
    pieces = refs[:MEMBERS]
    own_ref, same_ref, cross_ref, again_ref, stack_ref, sum_ref, sems = refs[MEMBERS:]
    virt = own_ref.shape[0]
    copies = [
        pltpu.make_async_copy(ref, stack_ref.at[pl.ds(d * virt, virt)], sems.at[d])
        for d, ref in enumerate(pieces)
    ]
    for copy in copies:
        copy.start()
    sum_ref[...] = jnp.zeros_like(sum_ref)

    def step(factors_ref, first):
        words = [plan_ref[first + i] for i in range(BATCH)]
        terms = []
        for word in words:
            start = pl.multiple_of(((word >> 8) & 15) * rows, rows)
            halves = [ref[(word >> 12) & 15, pl.ds(start, rows), :] for ref in (blocks_ref, others_ref)]
            terms.append(
                lax.dot_general(
                    jnp.concatenate(halves),
                    factors_ref[word & 15],
                    (((1,), (1,)), ((), ())),
                    preferred_element_type=jnp.float32,
                )
            )
        for word, term in zip(words, terms):
            sum_ref[(word >> 4) & 15] += term

    picks = [(place_ref[0] ^ d, ref) for d, ref in enumerate(pieces)]
    over_slots(plan_ref, owners, picks, step)
    own = sum_ref[pl.ds(0, virt), pl.ds(0, rows), :]
    own_ref[...] = own
    same_ref[...] = own.astype(same_ref.dtype)
    cross = sum_ref[pl.ds(0, virt), pl.ds(rows, rows), :].astype(cross_ref.dtype)
    cross_ref[...] = cross
    again_ref[...] = cross
    for copy in copies:
        copy.wait()


def contract(place, listed, blocks, others, factors, owners, virt, rows):
    chunk, depth = factors[0].shape[1:]
    sent = jax.ShapeDtypeStruct((virt, rows, chunk), jnp.bfloat16)
    stack = jax.ShapeDtypeStruct((MEMBERS * virt, chunk, depth), jnp.bfloat16)
    return pl.pallas_call(
        lambda *refs: contract_kernel(owners, rows, *refs),
        out_shape=(jax.ShapeDtypeStruct((virt, rows, chunk), jnp.float32), sent, sent, sent, stack),
        in_specs=[SMEM_SPEC] * 2 + [VMEM_SPEC] * (2 + len(factors)),
        out_specs=(VMEM_SPEC,) * 4 + (pl.BlockSpec(memory_space=pl.ANY),),
        scratch_shapes=[
            pltpu.VMEM((virt + 1, 2 * rows, chunk), jnp.float32),
            pltpu.SemaphoreType.DMA((MEMBERS,)),
        ],
        compiler_params=PARAMS,
        cost_estimate=cost("contract"),
        name="contract",
    )(place, listed, blocks, others, *factors)


def whole_kernel(owners, rows, virt, plan_ref, blocks_ref, *refs):
    out_ref, sum_ref, inter_ref = refs[-3:]
    factors_ref = refs[0]
    so_far = refs[1:-3]
    out_ref[...] = so_far[0][...] if so_far else jnp.zeros_like(out_ref)
    sum_ref[...] = jnp.zeros_like(sum_ref)
    picks = [(k, factors_ref.at[pl.ds(k * virt, virt)]) for k in range(owners)]
    over_slots(plan_ref, owners, picks, add_blocks(plan_ref, blocks_ref, rows, sum_ref))
    inter_ref[...] = sum_ref[...].astype(inter_ref.dtype)
    over_slots(plan_ref, owners, picks, add_products(plan_ref, inter_ref, out_ref))


def whole(listed, blocks, factors, so_far, owners, virt, rows, total):
    chunk, depth = factors.shape[1:]
    so_far = [] if so_far is None else [so_far]
    return pl.pallas_call(
        lambda *refs: whole_kernel(owners, rows, virt, *refs),
        out_shape=jax.ShapeDtypeStruct((total + 1, rows, depth), jnp.float32),
        in_specs=[SMEM_SPEC] + [VMEM_SPEC] * (2 + len(so_far)),
        out_specs=VMEM_SPEC,
        scratch_shapes=[
            pltpu.VMEM((virt + 1, rows, chunk), jnp.float32),
            pltpu.VMEM((virt + 1, rows, chunk), jnp.bfloat16),
        ],
        compiler_params=PARAMS,
        cost_estimate=cost("whole"),
        name="whole",
    )(listed, blocks, factors, *so_far)


def project_kernel(owners, place_ref, plan_ref, own_ref, got_ref, so_far_ref, *refs):
    out_ref, inter_ref = refs[-2:]
    virt = got_ref.shape[0]
    summed = own_ref[...].astype(jnp.float32) + got_ref[...].astype(jnp.float32)
    inter_ref[pl.ds(0, virt)] = summed.astype(inter_ref.dtype)
    inter_ref[virt] = jnp.zeros(inter_ref.shape[1:], inter_ref.dtype)
    out_ref[...] = so_far_ref[...]
    pieces = refs[:-2]
    if len(pieces) == 1:
        pieces = [refs[0].at[pl.ds(d * virt, virt)] for d in range(MEMBERS)]
    picks = [(place_ref[0] ^ d, ref) for d, ref in enumerate(pieces)]
    over_slots(plan_ref, owners, picks, add_products(plan_ref, inter_ref, out_ref))


def project(place, listed, own, got, factors, so_far, owners):
    virt, rows, chunk = got.shape
    return pl.pallas_call(
        lambda *refs: project_kernel(owners, *refs),
        out_shape=jax.ShapeDtypeStruct(so_far.shape, jnp.float32),
        in_specs=[SMEM_SPEC] * 2 + [VMEM_SPEC] * (3 + len(factors)),
        out_specs=VMEM_SPEC,
        scratch_shapes=[pltpu.VMEM((virt + 1, rows, chunk), jnp.bfloat16)],
        compiler_params=PARAMS,
        cost_estimate=cost("project"),
        name="project",
    )(place, listed, own, got, so_far, *factors)


def touch(values, *others):
    values = list(values)
    anywhere = pl.BlockSpec(memory_space=pl.ANY)
    return pl.pallas_call(
        lambda *refs: None,
        out_shape=[jax.ShapeDtypeStruct(value.shape, value.dtype) for value in values],
        in_specs=[anywhere] * (len(values) + len(others)),
        out_specs=[anywhere] * len(values),
        input_output_aliases={i: i for i in range(len(values))},
        name="touch",
    )(*values, *others)


def gather_kernel(place_ref, *refs):
    out_ref = refs[-1]
    shares = len(refs) - 1
    rows = out_ref.shape[1] // shares
    for a, ref in enumerate(refs[:-1]):
        share = place_ref[0] ^ a
        start = ((share & 1) * (shares // 2) + (share >> 1)) * rows
        out_ref[:, pl.ds(pl.multiple_of(start, rows), rows), :] = ref[...]


def gather(share, pieces):
    slots, rows, depth = pieces[0].shape
    return pl.pallas_call(
        gather_kernel,
        out_shape=jax.ShapeDtypeStruct((slots, rows * len(pieces), depth), pieces[0].dtype),
        in_specs=[SMEM_SPEC] + [VMEM_SPEC] * len(pieces),
        out_specs=VMEM_SPEC,
        compiler_params=PARAMS,
        name="gather",
    )(share.reshape(1).astype(jnp.int32), *pieces)


def after(value, *others):
    return lax.optimization_barrier((value, *others))[0]


def near_plan(factors, amplitudes, block_list, owner_map):
    pairs = lax.axis_size("pair")
    shares = lax.axis_size("aux")
    wide = shares // 2
    me = lax.axis_index("pair")
    share = lax.axis_index("aux")
    half, part = share & 1, share >> 1
    place = jnp.stack([me, half]).astype(jnp.int32)
    slots, width, depth = amplitudes.shape
    rows = width // 2
    total = pairs * slots
    virt = factors.shape[2]
    factors = factors[0]
    full_rows = factors.shape[0] // FULL
    full_chunk = full_rows // pairs
    chunk = (factors.shape[0] - full_rows) // MEMBERS

    def over_pair(value, distance):
        if distance == 0:
            return value
        return lax.ppermute(value, "pair", [(i, i ^ distance) for i in range(pairs)])

    def over_aux(value, distance):
        return lax.ppermute(value, "aux", [(i, i ^ distance) for i in range(shares)])

    def over_both(value, far, near):
        route = [
            (i * shares + k, (i ^ far) * shares + (k ^ near))
            for i in range(pairs)
            for k in range(shares)
        ]
        return lax.ppermute(value, ("pair", "aux"), route)

    full = factors[:full_rows].reshape(pairs, full_chunk, virt, depth)
    full, turn = lax.optimization_barrier((full, me))
    starts = [full_rows + ((turn & (MEMBERS - 1)) ^ d) * chunk for d in range(MEMBERS)]
    pieces = [lax.dynamic_slice_in_dim(factors, start, chunk, 0) for start in starts]
    pieces = [jnp.transpose(piece, (1, 0, 2)) for piece in pieces]

    packed = pack(place, block_list, owner_map, after(amplitudes, turn))
    near = jnp.stack([over_pair(packed, 2 * i) for i in range(pairs // 2)])
    blocks = jnp.concatenate([near, over_pair(near, 1)])
    meta = blocks[:, slots * rows : slots * rows + slots, :3].astype(jnp.int32)
    listed = plan(meta.reshape(total, 3), slots, pairs, virt)

    full = lax.all_to_all(touch([jnp.transpose(full, (0, 2, 1, 3))], near)[0], "pair", 0, 0, tiled=True)
    for d in (3,):
        pieces[d] = after(pieces[d], near)

    others = over_aux(blocks, 1)
    mine = [over_pair(pieces[d], d) for d in range(1, MEMBERS)]
    mine = [pieces[0], *touch(mine, listed, others)]
    own, same, cross, again, stack = contract(place, listed, blocks, others, mine, pairs, virt, rows)
    got = over_pair(same, MEMBERS), over_both(cross, MEMBERS, 1)
    own = own, over_aux(again, 1)
    work = list(zip(own, got, (mine, [over_aux(stack, 1)])))
    full = after(full, same).reshape(pairs * virt, full_chunk, depth)
    out = None
    for held in (full, over_aux(full, 1)):
        out = whole(listed, blocks, held, out, pairs, virt, rows, total)
    for own, got, held in work:
        out = project(place, listed, own, got, held, out, pairs)

    quarter = rows // wide
    out = out[:total].reshape(2, pairs // 2, slots, wide, quarter, depth)
    summed = None
    for h in range(wide):
        piece = lax.dynamic_index_in_dim(out, part ^ h, 3, False)
        for y in range(2):
            value = piece[y]
            if (y, h) != (0, 0):
                value = over_both(value.astype(jnp.bfloat16), y, 2 * h).astype(jnp.float32)
            summed = value if summed is None else summed + value
    summed = summed.astype(jnp.bfloat16)
    home = None
    for i in range(pairs // 2):
        value = over_pair(summed[i], 2 * i).astype(jnp.float32)
        home = value if home is None else home + value
    result = home.astype(jnp.bfloat16)
    return gather(share, [result] + [over_aux(result, a) for a in range(1, shares)])


def far_plan(factors, amplitudes, block_list, owner_map):
    pair_count = lax.axis_size("pair")
    slot_total = pair_count * CAP
    block_count = amplitudes.shape[0]
    block_width = amplitudes.shape[1]
    virt_blocks = factors.shape[2]
    share_rows = factors.shape[1]
    orbital_total = owner_map.shape[0]
    orbitals = block_list[:, 0]
    block_a = block_list[:, 1]
    block_c = block_list[:, 2]
    matches = orbitals[:, None] == lax.iota(jnp.int32, orbital_total)[None, :]
    owners = jnp.sum(jnp.where(matches, owner_map[None, :], 0), axis=1)
    owner_hits = (owners[:, None] == lax.iota(jnp.int32, pair_count)[None, :]).astype(jnp.int32)
    earlier = jnp.cumsum(owner_hits, axis=0) - owner_hits
    slot_rank = jnp.sum(earlier * owner_hits, axis=1)
    slots = owners * CAP + slot_rank
    placing = slots[:, None] == lax.iota(jnp.int32, slot_total)[None, :]
    place_matrix = placing.astype(jnp.bfloat16)
    flat_blocks = amplitudes.reshape(block_count, block_width * block_width)
    send_blocks = jnp.einsum(
        "js,jm->sm", place_matrix, flat_blocks, preferred_element_type=jnp.float32
    )
    send_blocks = send_blocks.astype(jnp.bfloat16).reshape(
        pair_count, CAP, block_width, block_width
    )
    send_a = jnp.sum(jnp.where(placing, block_a[:, None] + 1, 0), axis=0)
    send_c = jnp.sum(jnp.where(placing, block_c[:, None] + 1, 0), axis=0)
    send_index = (
        jnp.stack([send_a, send_c], axis=-1).astype(jnp.bfloat16).reshape(pair_count, CAP, 2)
    )
    recv_blocks, recv_index = (
        lax.all_to_all(send_blocks, "pair", split_axis=0, concat_axis=0, tiled=True),
        lax.all_to_all(send_index, "pair", split_axis=0, concat_axis=0, tiled=True),
    )
    recv_index = recv_index.reshape(slot_total, 2).astype(jnp.int32) - 1
    slot_a = recv_index[:, 0]
    slot_c = recv_index[:, 1]
    onehot_a = (slot_a[:, None] == lax.iota(jnp.int32, virt_blocks)[None, :]).astype(jnp.bfloat16)
    onehot_c = (slot_c[:, None] == lax.iota(jnp.int32, virt_blocks)[None, :]).astype(jnp.bfloat16)
    combined = (onehot_c[:, :, None] * onehot_a[:, None, :]).reshape(
        slot_total, virt_blocks * virt_blocks
    )
    recv_flat = recv_blocks.reshape(slot_total, block_width * block_width)
    weights = jnp.einsum("sm,sn->mn", combined, recv_flat, preferred_element_type=jnp.float32)
    weights = weights.reshape(virt_blocks, virt_blocks, block_width, block_width)
    weights = jnp.transpose(weights, (0, 3, 1, 2)).reshape(
        virt_blocks * block_width, virt_blocks * block_width
    )
    weights = weights.astype(jnp.bfloat16)
    factor_flat = factors.reshape(share_rows, virt_blocks * block_width)
    factor_rows = factor_flat
    inter_share = lax.psum_scatter(
        jnp.dot(factor_rows, weights, preferred_element_type=jnp.float32),
        "pair",
        scatter_dimension=0,
        tiled=True,
    )
    inter_share = inter_share.astype(jnp.bfloat16)
    shard_rows = lax.all_gather(inter_share, "pair", axis=0, tiled=True)
    height = shard_rows.shape[0]
    factor_rows = factor_flat
    left = shard_rows.reshape(height, virt_blocks, block_width)
    right = factor_rows.reshape(height, virt_blocks, block_width)
    projected = jnp.einsum("qAa,qCc->ACac", left, right, preferred_element_type=jnp.float32)
    safe_a = jnp.maximum(slot_a, 0)
    safe_c = jnp.maximum(slot_c, 0)
    summed = lax.psum(projected, "aux")
    picked = summed[safe_a, safe_c].astype(jnp.bfloat16)
    picked = picked.reshape(pair_count, CAP, block_width, block_width)
    returned = lax.all_to_all(picked, "pair", split_axis=0, concat_axis=0, tiled=True)
    returned = returned.reshape(slot_total, block_width * block_width)
    result = jnp.einsum("js,sm->jm", place_matrix, returned, preferred_element_type=jnp.float32)
    return result.astype(jnp.bfloat16).reshape(block_count, block_width, block_width)


def on_device(factors, amplitudes, block_list, owner_map):
    fits = amplitudes.shape[0] < META and factors.shape[2] < META
    plan_of = near_plan if lax.axis_size("pair") == 2 * MEMBERS and fits else far_plan
    return plan_of(factors, amplitudes, block_list, owner_map)


def solution(mesh):
    placed = (P("pair", "aux", None, None), P("pair", None, None), P("pair", None), P())
    return jax.shard_map(
        on_device, mesh=mesh, in_specs=placed, out_specs=P("pair", None, None), check_vma=False
    )
```

```python
import jax
import jax.numpy as jnp
from jax import lax
from jax.experimental import pallas as pl
from jax.experimental.pallas import tpu as pltpu
from jax.sharding import PartitionSpec as P

CAP = 2
BATCH = 6
META = 16
MEMBERS = 4
FULL = 2
VMEM_BYTES = 16 * 1024 * 1024

SMEM_SPEC = pl.BlockSpec(memory_space=pltpu.SMEM)
VMEM_SPEC = pl.BlockSpec(memory_space=pltpu.VMEM)
PARAMS = pltpu.CompilerParams(vmem_limit_bytes=VMEM_BYTES)
COSTS = dict(pack=0, plan=10**13, contract=10**13, whole=0, project=0)


def cost(name):
    return pl.CostEstimate(flops=COSTS[name], bytes_accessed=0, transcendentals=0)


def pack_kernel(place_ref, list_ref, owner_ref, blocks_ref, out_ref):
    half = place_ref[1]
    count, width, depth = blocks_ref.shape
    rows = width // 2
    line = lax.broadcasted_iota(jnp.int32, (META, depth), 0)
    lane = lax.broadcasted_iota(jnp.int32, (META, depth), 1)
    meta = jnp.zeros((META, depth), jnp.float32)
    taken = pl.ds(pl.multiple_of(half * rows, rows), rows)
    for j in range(count):
        out_ref[j * rows : (j + 1) * rows, :] = blocks_ref[j, taken, :]
        owner = owner_ref[list_ref[j, 0]]
        for k, value in enumerate((list_ref[j, 1], list_ref[j, 2], owner)):
            meta = jnp.where((line == j) & (lane == k), value.astype(jnp.float32), meta)
    out_ref[pl.ds(count * rows, META), :] = meta.astype(out_ref.dtype)


def pack(place, block_list, owner_map, blocks):
    count, width, depth = blocks.shape
    return pl.pallas_call(
        pack_kernel,
        out_shape=jax.ShapeDtypeStruct((count * (width // 2) + META, depth), blocks.dtype),
        in_specs=[SMEM_SPEC, SMEM_SPEC, SMEM_SPEC, VMEM_SPEC],
        out_specs=VMEM_SPEC,
        compiler_params=PARAMS,
        cost_estimate=cost("pack"),
        name="pack",
    )(place, block_list, owner_map, blocks)


def plan_kernel(slots, owners, virt, meta_ref, out_ref, filled_ref):
    total = meta_ref.shape[0]
    room = total + BATCH
    for m in range(owners):
        filled_ref[m] = m * room

    def one(s, place):
        owner = meta_ref[s, 2]
        sender, first = place
        where = meta_ref[s, 0] * 16 + meta_ref[s, 1]
        at = filled_ref[owner]
        out_ref[at] = ((s * 16 + sender) * 16 + s - first) * 256 + where
        filled_ref[owner] = at + 1
        over = s + 1 - first == slots
        return sender + over.astype(jnp.int32), jnp.where(over, s + 1, first)

    lax.fori_loop(0, total, one, (jnp.int32(0), jnp.int32(0)))
    for m in range(owners):
        n = filled_ref[m]
        for u in range(BATCH):
            out_ref[n + u] = jnp.int32(total * 65536 + virt * 16)
        out_ref[owners * room + m] = lax.div(n - m * room + BATCH - 1, BATCH)


def plan(meta, slots, owners, virt):
    room = meta.shape[0] + BATCH
    return pl.pallas_call(
        lambda *refs: plan_kernel(slots, owners, virt, *refs),
        out_shape=jax.ShapeDtypeStruct((owners * room + owners,), jnp.int32),
        in_specs=[SMEM_SPEC],
        out_specs=SMEM_SPEC,
        scratch_shapes=[pltpu.SMEM((owners,), jnp.int32)],
        cost_estimate=cost("plan"),
        name="plan",
    )(meta)


def over_slots(plan_ref, owners, picks, step):
    room = plan_ref.shape[0] // owners - 1
    for owner, ref in picks:

        def batch(b, carry, owner=owner, ref=ref):
            step(ref, owner * room + b * BATCH)
            return carry

        lax.fori_loop(0, plan_ref[owners * room + owner], batch, 0)


def add_blocks(plan_ref, blocks_ref, rows, sum_ref):
    def step(factors_ref, first):
        words = [plan_ref[first + i] for i in range(BATCH)]
        terms = []
        for word in words:
            start = pl.multiple_of(((word >> 8) & 15) * rows, rows)
            terms.append(
                lax.dot_general(
                    blocks_ref[(word >> 12) & 15, pl.ds(start, rows), :],
                    factors_ref[word & 15],
                    (((1,), (1,)), ((), ())),
                    preferred_element_type=jnp.float32,
                )
            )
        for word, term in zip(words, terms):
            sum_ref[(word >> 4) & 15] += term

    return step


def add_products(plan_ref, inter_ref, out_ref):
    def step(factors_ref, first):
        words = [plan_ref[first + i] for i in range(BATCH)]
        terms = []
        for word in words:
            terms.append(
                jnp.dot(
                    inter_ref[(word >> 4) & 15],
                    factors_ref[word & 15],
                    preferred_element_type=jnp.float32,
                )
            )
        for word, term in zip(words, terms):
            out_ref[word >> 16] += term

    return step


def contract_kernel(owners, rows, place_ref, plan_ref, blocks_ref, others_ref, *refs):
    pieces = refs[:MEMBERS]
    own_ref, same_ref, cross_ref, again_ref, stack_ref, sum_ref, sems = refs[MEMBERS:]
    virt = own_ref.shape[0]
    copies = [
        pltpu.make_async_copy(ref, stack_ref.at[pl.ds(d * virt, virt)], sems.at[d])
        for d, ref in enumerate(pieces)
    ]
    for copy in copies:
        copy.start()
    sum_ref[...] = jnp.zeros_like(sum_ref)

    def step(factors_ref, first):
        words = [plan_ref[first + i] for i in range(BATCH)]
        terms = []
        for word in words:
            start = pl.multiple_of(((word >> 8) & 15) * rows, rows)
            halves = [ref[(word >> 12) & 15, pl.ds(start, rows), :] for ref in (blocks_ref, others_ref)]
            terms.append(
                lax.dot_general(
                    jnp.concatenate(halves),
                    factors_ref[word & 15],
                    (((1,), (1,)), ((), ())),
                    preferred_element_type=jnp.float32,
                )
            )
        for word, term in zip(words, terms):
            sum_ref[(word >> 4) & 15] += term

    picks = [(place_ref[0] ^ d, ref) for d, ref in enumerate(pieces)]
    over_slots(plan_ref, owners, picks, step)
    own = sum_ref[pl.ds(0, virt), pl.ds(0, rows), :]
    own_ref[...] = own
    same_ref[...] = own.astype(same_ref.dtype)
    cross = sum_ref[pl.ds(0, virt), pl.ds(rows, rows), :].astype(cross_ref.dtype)
    cross_ref[...] = cross
    again_ref[...] = cross
    for copy in copies:
        copy.wait()


def contract(place, listed, blocks, others, factors, owners, virt, rows):
    chunk, depth = factors[0].shape[1:]
    sent = jax.ShapeDtypeStruct((virt, rows, chunk), jnp.bfloat16)
    stack = jax.ShapeDtypeStruct((MEMBERS * virt, chunk, depth), jnp.bfloat16)
    return pl.pallas_call(
        lambda *refs: contract_kernel(owners, rows, *refs),
        out_shape=(jax.ShapeDtypeStruct((virt, rows, chunk), jnp.float32), sent, sent, sent, stack),
        in_specs=[SMEM_SPEC] * 2 + [VMEM_SPEC] * (2 + len(factors)),
        out_specs=(VMEM_SPEC,) * 4 + (pl.BlockSpec(memory_space=pl.ANY),),
        scratch_shapes=[
            pltpu.VMEM((virt + 1, 2 * rows, chunk), jnp.float32),
            pltpu.SemaphoreType.DMA((MEMBERS,)),
        ],
        compiler_params=PARAMS,
        cost_estimate=cost("contract"),
        name="contract",
    )(place, listed, blocks, others, *factors)


def whole_kernel(owners, rows, virt, plan_ref, blocks_ref, *refs):
    out_ref, sum_ref, inter_ref = refs[-3:]
    factors_ref = refs[0]
    so_far = refs[1:-3]
    out_ref[...] = so_far[0][...] if so_far else jnp.zeros_like(out_ref)
    sum_ref[...] = jnp.zeros_like(sum_ref)
    picks = [(k, factors_ref.at[pl.ds(k * virt, virt)]) for k in range(owners)]
    over_slots(plan_ref, owners, picks, add_blocks(plan_ref, blocks_ref, rows, sum_ref))
    inter_ref[...] = sum_ref[...].astype(inter_ref.dtype)
    over_slots(plan_ref, owners, picks, add_products(plan_ref, inter_ref, out_ref))


def whole(listed, blocks, factors, so_far, owners, virt, rows, total):
    chunk, depth = factors.shape[1:]
    so_far = [] if so_far is None else [so_far]
    return pl.pallas_call(
        lambda *refs: whole_kernel(owners, rows, virt, *refs),
        out_shape=jax.ShapeDtypeStruct((total + 1, rows, depth), jnp.float32),
        in_specs=[SMEM_SPEC] + [VMEM_SPEC] * (2 + len(so_far)),
        out_specs=VMEM_SPEC,
        scratch_shapes=[
            pltpu.VMEM((virt + 1, rows, chunk), jnp.float32),
            pltpu.VMEM((virt + 1, rows, chunk), jnp.bfloat16),
        ],
        compiler_params=PARAMS,
        cost_estimate=cost("whole"),
        name="whole",
    )(listed, blocks, factors, *so_far)


def project_kernel(owners, place_ref, plan_ref, own_ref, got_ref, so_far_ref, *refs):
    out_ref, inter_ref = refs[-2:]
    virt = got_ref.shape[0]
    summed = own_ref[...].astype(jnp.float32) + got_ref[...].astype(jnp.float32)
    inter_ref[pl.ds(0, virt)] = summed.astype(inter_ref.dtype)
    inter_ref[virt] = jnp.zeros(inter_ref.shape[1:], inter_ref.dtype)
    out_ref[...] = so_far_ref[...]
    pieces = refs[:-2]
    if len(pieces) == 1:
        pieces = [refs[0].at[pl.ds(d * virt, virt)] for d in range(MEMBERS)]
    picks = [(place_ref[0] ^ d, ref) for d, ref in enumerate(pieces)]
    over_slots(plan_ref, owners, picks, add_products(plan_ref, inter_ref, out_ref))


def project(place, listed, own, got, factors, so_far, owners):
    virt, rows, chunk = got.shape
    return pl.pallas_call(
        lambda *refs: project_kernel(owners, *refs),
        out_shape=jax.ShapeDtypeStruct(so_far.shape, jnp.float32),
        in_specs=[SMEM_SPEC] * 2 + [VMEM_SPEC] * (3 + len(factors)),
        out_specs=VMEM_SPEC,
        scratch_shapes=[pltpu.VMEM((virt + 1, rows, chunk), jnp.bfloat16)],
        compiler_params=PARAMS,
        cost_estimate=cost("project"),
        name="project",
    )(place, listed, own, got, so_far, *factors)


def touch(values, *others):
    values = list(values)
    anywhere = pl.BlockSpec(memory_space=pl.ANY)
    return pl.pallas_call(
        lambda *refs: None,
        out_shape=[jax.ShapeDtypeStruct(value.shape, value.dtype) for value in values],
        in_specs=[anywhere] * (len(values) + len(others)),
        out_specs=[anywhere] * len(values),
        input_output_aliases={i: i for i in range(len(values))},
        name="touch",
    )(*values, *others)


def gather_kernel(place_ref, *refs):
    out_ref = refs[-1]
    shares = len(refs) - 1
    rows = out_ref.shape[1] // shares
    for a, ref in enumerate(refs[:-1]):
        share = place_ref[0] ^ a
        start = ((share & 1) * (shares // 2) + (share >> 1)) * rows
        out_ref[:, pl.ds(pl.multiple_of(start, rows), rows), :] = ref[...]


def gather(share, pieces):
    slots, rows, depth = pieces[0].shape
    return pl.pallas_call(
        gather_kernel,
        out_shape=jax.ShapeDtypeStruct((slots, rows * len(pieces), depth), pieces[0].dtype),
        in_specs=[SMEM_SPEC] + [VMEM_SPEC] * len(pieces),
        out_specs=VMEM_SPEC,
        compiler_params=PARAMS,
        name="gather",
    )(share.reshape(1).astype(jnp.int32), *pieces)


def after(value, *others):
    return lax.optimization_barrier((value, *others))[0]


def near_plan(factors, amplitudes, block_list, owner_map):
    pairs = lax.axis_size("pair")
    shares = lax.axis_size("aux")
    wide = shares // 2
    me = lax.axis_index("pair")
    share = lax.axis_index("aux")
    half, part = share & 1, share >> 1
    place = jnp.stack([me, half]).astype(jnp.int32)
    slots, width, depth = amplitudes.shape
    rows = width // 2
    total = pairs * slots
    virt = factors.shape[2]
    factors = factors[0]
    full_rows = factors.shape[0] // FULL
    full_chunk = full_rows // pairs
    chunk = (factors.shape[0] - full_rows) // MEMBERS

    def over_pair(value, distance):
        if distance == 0:
            return value
        return lax.ppermute(value, "pair", [(i, i ^ distance) for i in range(pairs)])

    def over_aux(value, distance):
        return lax.ppermute(value, "aux", [(i, i ^ distance) for i in range(shares)])

    def over_both(value, far, near):
        route = [
            (i * shares + k, (i ^ far) * shares + (k ^ near))
            for i in range(pairs)
            for k in range(shares)
        ]
        return lax.ppermute(value, ("pair", "aux"), route)

    full = factors[:full_rows].reshape(pairs, full_chunk, virt, depth)
    full, turn = lax.optimization_barrier((full, me))
    starts = [full_rows + ((turn & (MEMBERS - 1)) ^ d) * chunk for d in range(MEMBERS)]
    pieces = [lax.dynamic_slice_in_dim(factors, start, chunk, 0) for start in starts]
    pieces = [jnp.transpose(piece, (1, 0, 2)) for piece in pieces]

    packed = pack(place, block_list, owner_map, after(amplitudes, turn))
    near = jnp.stack([over_pair(packed, 2 * i) for i in range(pairs // 2)])
    blocks = jnp.concatenate([near, over_pair(near, 1)])
    meta = blocks[:, slots * rows : slots * rows + slots, :3].astype(jnp.int32)
    listed = plan(meta.reshape(total, 3), slots, pairs, virt)

    full = lax.all_to_all(touch([jnp.transpose(full, (0, 2, 1, 3))], near)[0], "pair", 0, 0, tiled=True)
    for d in (2,):
        pieces[d] = after(pieces[d], near)

    others = over_aux(blocks, 1)
    mine = [over_pair(pieces[d], d) for d in range(1, MEMBERS)]
    mine = [pieces[0], *touch(mine, listed, others)]
    own, same, cross, again, stack = contract(place, listed, blocks, others, mine, pairs, virt, rows)
    got = over_pair(same, MEMBERS), over_both(cross, MEMBERS, 1)
    own = own, over_aux(again, 1)
    work = list(zip(own, got, (mine, [over_aux(stack, 1)])))
    full = after(full, same).reshape(pairs * virt, full_chunk, depth)
    out = None
    for held in (full, over_aux(full, 1)):
        out = whole(listed, blocks, held, out, pairs, virt, rows, total)
    for own, got, held in work:
        out = project(place, listed, own, got, held, out, pairs)

    quarter = rows // wide
    out = out[:total].reshape(2, pairs // 2, slots, wide, quarter, depth)
    summed = None
    for h in range(wide):
        piece = lax.dynamic_index_in_dim(out, part ^ h, 3, False)
        for y in range(2):
            value = piece[y]
            if (y, h) != (0, 0):
                value = over_both(value.astype(jnp.bfloat16), y, 2 * h).astype(jnp.float32)
            summed = value if summed is None else summed + value
    summed = summed.astype(jnp.bfloat16)
    home = None
    for i in range(pairs // 2):
        value = over_pair(summed[i], 2 * i).astype(jnp.float32)
        home = value if home is None else home + value
    result = home.astype(jnp.bfloat16)
    return gather(share, [result] + [over_aux(result, a) for a in range(1, shares)])


def far_plan(factors, amplitudes, block_list, owner_map):
    pair_count = lax.axis_size("pair")
    slot_total = pair_count * CAP
    block_count = amplitudes.shape[0]
    block_width = amplitudes.shape[1]
    virt_blocks = factors.shape[2]
    share_rows = factors.shape[1]
    orbital_total = owner_map.shape[0]
    orbitals = block_list[:, 0]
    block_a = block_list[:, 1]
    block_c = block_list[:, 2]
    matches = orbitals[:, None] == lax.iota(jnp.int32, orbital_total)[None, :]
    owners = jnp.sum(jnp.where(matches, owner_map[None, :], 0), axis=1)
    owner_hits = (owners[:, None] == lax.iota(jnp.int32, pair_count)[None, :]).astype(jnp.int32)
    earlier = jnp.cumsum(owner_hits, axis=0) - owner_hits
    slot_rank = jnp.sum(earlier * owner_hits, axis=1)
    slots = owners * CAP + slot_rank
    placing = slots[:, None] == lax.iota(jnp.int32, slot_total)[None, :]
    place_matrix = placing.astype(jnp.bfloat16)
    flat_blocks = amplitudes.reshape(block_count, block_width * block_width)
    send_blocks = jnp.einsum(
        "js,jm->sm", place_matrix, flat_blocks, preferred_element_type=jnp.float32
    )
    send_blocks = send_blocks.astype(jnp.bfloat16).reshape(
        pair_count, CAP, block_width, block_width
    )
    send_a = jnp.sum(jnp.where(placing, block_a[:, None] + 1, 0), axis=0)
    send_c = jnp.sum(jnp.where(placing, block_c[:, None] + 1, 0), axis=0)
    send_index = (
        jnp.stack([send_a, send_c], axis=-1).astype(jnp.bfloat16).reshape(pair_count, CAP, 2)
    )
    recv_blocks, recv_index = (
        lax.all_to_all(send_blocks, "pair", split_axis=0, concat_axis=0, tiled=True),
        lax.all_to_all(send_index, "pair", split_axis=0, concat_axis=0, tiled=True),
    )
    recv_index = recv_index.reshape(slot_total, 2).astype(jnp.int32) - 1
    slot_a = recv_index[:, 0]
    slot_c = recv_index[:, 1]
    onehot_a = (slot_a[:, None] == lax.iota(jnp.int32, virt_blocks)[None, :]).astype(jnp.bfloat16)
    onehot_c = (slot_c[:, None] == lax.iota(jnp.int32, virt_blocks)[None, :]).astype(jnp.bfloat16)
    combined = (onehot_c[:, :, None] * onehot_a[:, None, :]).reshape(
        slot_total, virt_blocks * virt_blocks
    )
    recv_flat = recv_blocks.reshape(slot_total, block_width * block_width)
    weights = jnp.einsum("sm,sn->mn", combined, recv_flat, preferred_element_type=jnp.float32)
    weights = weights.reshape(virt_blocks, virt_blocks, block_width, block_width)
    weights = jnp.transpose(weights, (0, 3, 1, 2)).reshape(
        virt_blocks * block_width, virt_blocks * block_width
    )
    weights = weights.astype(jnp.bfloat16)
    factor_flat = factors.reshape(share_rows, virt_blocks * block_width)
    factor_rows = factor_flat
    inter_share = lax.psum_scatter(
        jnp.dot(factor_rows, weights, preferred_element_type=jnp.float32),
        "pair",
        scatter_dimension=0,
        tiled=True,
    )
    inter_share = inter_share.astype(jnp.bfloat16)
    shard_rows = lax.all_gather(inter_share, "pair", axis=0, tiled=True)
    height = shard_rows.shape[0]
    factor_rows = factor_flat
    left = shard_rows.reshape(height, virt_blocks, block_width)
    right = factor_rows.reshape(height, virt_blocks, block_width)
    projected = jnp.einsum("qAa,qCc->ACac", left, right, preferred_element_type=jnp.float32)
    safe_a = jnp.maximum(slot_a, 0)
    safe_c = jnp.maximum(slot_c, 0)
    summed = lax.psum(projected, "aux")
    picked = summed[safe_a, safe_c].astype(jnp.bfloat16)
    picked = picked.reshape(pair_count, CAP, block_width, block_width)
    returned = lax.all_to_all(picked, "pair", split_axis=0, concat_axis=0, tiled=True)
    returned = returned.reshape(slot_total, block_width * block_width)
    result = jnp.einsum("js,sm->jm", place_matrix, returned, preferred_element_type=jnp.float32)
    return result.astype(jnp.bfloat16).reshape(block_count, block_width, block_width)


def on_device(factors, amplitudes, block_list, owner_map):
    fits = amplitudes.shape[0] < META and factors.shape[2] < META
    plan_of = near_plan if lax.axis_size("pair") == 2 * MEMBERS and fits else far_plan
    return plan_of(factors, amplitudes, block_list, owner_map)


def solution(mesh):
    placed = (P("pair", "aux", None, None), P("pair", None, None), P("pair", None), P())
    return jax.shard_map(
        on_device, mesh=mesh, in_specs=placed, out_specs=P("pair", None, None), check_vma=False
    )
```

```python
import jax
import jax.numpy as jnp
from jax import lax
from jax.experimental import pallas as pl
from jax.experimental.pallas import tpu as pltpu
from jax.sharding import PartitionSpec as P

CAP = 2
BATCH = 6
META = 16
MEMBERS = 4
FULL = 2
VMEM_BYTES = 16 * 1024 * 1024

SMEM_SPEC = pl.BlockSpec(memory_space=pltpu.SMEM)
VMEM_SPEC = pl.BlockSpec(memory_space=pltpu.VMEM)
PARAMS = pltpu.CompilerParams(vmem_limit_bytes=VMEM_BYTES)
COSTS = dict(pack=0, plan=10**13, contract=10**13, whole=0, project=0)


def cost(name):
    return pl.CostEstimate(flops=COSTS[name], bytes_accessed=0, transcendentals=0)


def pack_kernel(place_ref, list_ref, owner_ref, blocks_ref, out_ref):
    half = place_ref[1]
    count, width, depth = blocks_ref.shape
    rows = width // 2
    line = lax.broadcasted_iota(jnp.int32, (META, depth), 0)
    lane = lax.broadcasted_iota(jnp.int32, (META, depth), 1)
    meta = jnp.zeros((META, depth), jnp.float32)
    taken = pl.ds(pl.multiple_of(half * rows, rows), rows)
    for j in range(count):
        out_ref[j * rows : (j + 1) * rows, :] = blocks_ref[j, taken, :]
        owner = owner_ref[list_ref[j, 0]]
        for k, value in enumerate((list_ref[j, 1], list_ref[j, 2], owner)):
            meta = jnp.where((line == j) & (lane == k), value.astype(jnp.float32), meta)
    out_ref[pl.ds(count * rows, META), :] = meta.astype(out_ref.dtype)


def pack(place, block_list, owner_map, blocks):
    count, width, depth = blocks.shape
    return pl.pallas_call(
        pack_kernel,
        out_shape=jax.ShapeDtypeStruct((count * (width // 2) + META, depth), blocks.dtype),
        in_specs=[SMEM_SPEC, SMEM_SPEC, SMEM_SPEC, VMEM_SPEC],
        out_specs=VMEM_SPEC,
        compiler_params=PARAMS,
        cost_estimate=cost("pack"),
        name="pack",
    )(place, block_list, owner_map, blocks)


def plan_kernel(slots, owners, virt, meta_ref, out_ref, filled_ref):
    total = meta_ref.shape[0]
    room = total + BATCH
    for m in range(owners):
        filled_ref[m] = m * room

    def one(s, place):
        owner = meta_ref[s, 2]
        sender, first = place
        where = meta_ref[s, 0] * 16 + meta_ref[s, 1]
        at = filled_ref[owner]
        out_ref[at] = ((s * 16 + sender) * 16 + s - first) * 256 + where
        filled_ref[owner] = at + 1
        over = s + 1 - first == slots
        return sender + over.astype(jnp.int32), jnp.where(over, s + 1, first)

    lax.fori_loop(0, total, one, (jnp.int32(0), jnp.int32(0)))
    for m in range(owners):
        n = filled_ref[m]
        for u in range(BATCH):
            out_ref[n + u] = jnp.int32(total * 65536 + virt * 16)
        out_ref[owners * room + m] = lax.div(n - m * room + BATCH - 1, BATCH)


def plan(meta, slots, owners, virt):
    room = meta.shape[0] + BATCH
    return pl.pallas_call(
        lambda *refs: plan_kernel(slots, owners, virt, *refs),
        out_shape=jax.ShapeDtypeStruct((owners * room + owners,), jnp.int32),
        in_specs=[SMEM_SPEC],
        out_specs=SMEM_SPEC,
        scratch_shapes=[pltpu.SMEM((owners,), jnp.int32)],
        cost_estimate=cost("plan"),
        name="plan",
    )(meta)


def over_slots(plan_ref, owners, picks, step):
    room = plan_ref.shape[0] // owners - 1
    for owner, ref in picks:

        def batch(b, carry, owner=owner, ref=ref):
            step(ref, owner * room + b * BATCH)
            return carry

        lax.fori_loop(0, plan_ref[owners * room + owner], batch, 0)


def add_blocks(plan_ref, blocks_ref, rows, sum_ref):
    def step(factors_ref, first):
        words = [plan_ref[first + i] for i in range(BATCH)]
        terms = []
        for word in words:
            start = pl.multiple_of(((word >> 8) & 15) * rows, rows)
            terms.append(
                lax.dot_general(
                    blocks_ref[(word >> 12) & 15, pl.ds(start, rows), :],
                    factors_ref[word & 15],
                    (((1,), (1,)), ((), ())),
                    preferred_element_type=jnp.float32,
                )
            )
        for word, term in zip(words, terms):
            sum_ref[(word >> 4) & 15] += term

    return step


def add_products(plan_ref, inter_ref, out_ref):
    def step(factors_ref, first):
        words = [plan_ref[first + i] for i in range(BATCH)]
        terms = []
        for word in words:
            terms.append(
                jnp.dot(
                    inter_ref[(word >> 4) & 15],
                    factors_ref[word & 15],
                    preferred_element_type=jnp.float32,
                )
            )
        for word, term in zip(words, terms):
            out_ref[word >> 16] += term

    return step


def contract_kernel(owners, rows, place_ref, plan_ref, blocks_ref, others_ref, *refs):
    pieces = refs[:MEMBERS]
    own_ref, same_ref, cross_ref, again_ref, stack_ref, sum_ref, sems = refs[MEMBERS:]
    virt = own_ref.shape[0]
    copies = [
        pltpu.make_async_copy(ref, stack_ref.at[pl.ds(d * virt, virt)], sems.at[d])
        for d, ref in enumerate(pieces)
    ]
    for copy in copies:
        copy.start()
    sum_ref[...] = jnp.zeros_like(sum_ref)

    def step(factors_ref, first):
        words = [plan_ref[first + i] for i in range(BATCH)]
        terms = []
        for word in words:
            start = pl.multiple_of(((word >> 8) & 15) * rows, rows)
            halves = [ref[(word >> 12) & 15, pl.ds(start, rows), :] for ref in (blocks_ref, others_ref)]
            terms.append(
                lax.dot_general(
                    jnp.concatenate(halves),
                    factors_ref[word & 15],
                    (((1,), (1,)), ((), ())),
                    preferred_element_type=jnp.float32,
                )
            )
        for word, term in zip(words, terms):
            sum_ref[(word >> 4) & 15] += term

    picks = [(place_ref[0] ^ d, ref) for d, ref in enumerate(pieces)]
    over_slots(plan_ref, owners, picks, step)
    own = sum_ref[pl.ds(0, virt), pl.ds(0, rows), :]
    own_ref[...] = own
    same_ref[...] = own.astype(same_ref.dtype)
    cross = sum_ref[pl.ds(0, virt), pl.ds(rows, rows), :].astype(cross_ref.dtype)
    cross_ref[...] = cross
    again_ref[...] = cross
    for copy in copies:
        copy.wait()


def contract(place, listed, blocks, others, factors, owners, virt, rows):
    chunk, depth = factors[0].shape[1:]
    sent = jax.ShapeDtypeStruct((virt, rows, chunk), jnp.bfloat16)
    stack = jax.ShapeDtypeStruct((MEMBERS * virt, chunk, depth), jnp.bfloat16)
    return pl.pallas_call(
        lambda *refs: contract_kernel(owners, rows, *refs),
        out_shape=(jax.ShapeDtypeStruct((virt, rows, chunk), jnp.float32), sent, sent, sent, stack),
        in_specs=[SMEM_SPEC] * 2 + [VMEM_SPEC] * (2 + len(factors)),
        out_specs=(VMEM_SPEC,) * 4 + (pl.BlockSpec(memory_space=pl.ANY),),
        scratch_shapes=[
            pltpu.VMEM((virt + 1, 2 * rows, chunk), jnp.float32),
            pltpu.SemaphoreType.DMA((MEMBERS,)),
        ],
        compiler_params=PARAMS,
        cost_estimate=cost("contract"),
        name="contract",
    )(place, listed, blocks, others, *factors)


def whole_kernel(owners, rows, virt, plan_ref, blocks_ref, *refs):
    out_ref, sum_ref, inter_ref = refs[-3:]
    factors_ref = refs[0]
    so_far = refs[1:-3]
    out_ref[...] = so_far[0][...] if so_far else jnp.zeros_like(out_ref)
    sum_ref[...] = jnp.zeros_like(sum_ref)
    picks = [(k, factors_ref.at[pl.ds(k * virt, virt)]) for k in range(owners)]
    over_slots(plan_ref, owners, picks, add_blocks(plan_ref, blocks_ref, rows, sum_ref))
    inter_ref[...] = sum_ref[...].astype(inter_ref.dtype)
    over_slots(plan_ref, owners, picks, add_products(plan_ref, inter_ref, out_ref))


def whole(listed, blocks, factors, so_far, owners, virt, rows, total):
    chunk, depth = factors.shape[1:]
    so_far = [] if so_far is None else [so_far]
    return pl.pallas_call(
        lambda *refs: whole_kernel(owners, rows, virt, *refs),
        out_shape=jax.ShapeDtypeStruct((total + 1, rows, depth), jnp.float32),
        in_specs=[SMEM_SPEC] + [VMEM_SPEC] * (2 + len(so_far)),
        out_specs=VMEM_SPEC,
        scratch_shapes=[
            pltpu.VMEM((virt + 1, rows, chunk), jnp.float32),
            pltpu.VMEM((virt + 1, rows, chunk), jnp.bfloat16),
        ],
        compiler_params=PARAMS,
        cost_estimate=cost("whole"),
        name="whole",
    )(listed, blocks, factors, *so_far)


def project_kernel(owners, place_ref, plan_ref, own_ref, got_ref, so_far_ref, *refs):
    out_ref, inter_ref = refs[-2:]
    virt = got_ref.shape[0]
    summed = own_ref[...].astype(jnp.float32) + got_ref[...].astype(jnp.float32)
    inter_ref[pl.ds(0, virt)] = summed.astype(inter_ref.dtype)
    inter_ref[virt] = jnp.zeros(inter_ref.shape[1:], inter_ref.dtype)
    out_ref[...] = so_far_ref[...]
    pieces = refs[:-2]
    if len(pieces) == 1:
        pieces = [refs[0].at[pl.ds(d * virt, virt)] for d in range(MEMBERS)]
    picks = [(place_ref[0] ^ d, ref) for d, ref in enumerate(pieces)]
    over_slots(plan_ref, owners, picks, add_products(plan_ref, inter_ref, out_ref))


def project(place, listed, own, got, factors, so_far, owners):
    virt, rows, chunk = got.shape
    return pl.pallas_call(
        lambda *refs: project_kernel(owners, *refs),
        out_shape=jax.ShapeDtypeStruct(so_far.shape, jnp.float32),
        in_specs=[SMEM_SPEC] * 2 + [VMEM_SPEC] * (3 + len(factors)),
        out_specs=VMEM_SPEC,
        scratch_shapes=[pltpu.VMEM((virt + 1, rows, chunk), jnp.bfloat16)],
        compiler_params=PARAMS,
        cost_estimate=cost("project"),
        name="project",
    )(place, listed, own, got, so_far, *factors)


def touch(values, *others):
    values = list(values)
    anywhere = pl.BlockSpec(memory_space=pl.ANY)
    return pl.pallas_call(
        lambda *refs: None,
        out_shape=[jax.ShapeDtypeStruct(value.shape, value.dtype) for value in values],
        in_specs=[anywhere] * (len(values) + len(others)),
        out_specs=[anywhere] * len(values),
        input_output_aliases={i: i for i in range(len(values))},
        name="touch",
    )(*values, *others)


def gather_kernel(place_ref, *refs):
    out_ref = refs[-1]
    shares = len(refs) - 1
    rows = out_ref.shape[1] // shares
    for a, ref in enumerate(refs[:-1]):
        share = place_ref[0] ^ a
        start = ((share & 1) * (shares // 2) + (share >> 1)) * rows
        out_ref[:, pl.ds(pl.multiple_of(start, rows), rows), :] = ref[...]


def gather(share, pieces):
    slots, rows, depth = pieces[0].shape
    return pl.pallas_call(
        gather_kernel,
        out_shape=jax.ShapeDtypeStruct((slots, rows * len(pieces), depth), pieces[0].dtype),
        in_specs=[SMEM_SPEC] + [VMEM_SPEC] * len(pieces),
        out_specs=VMEM_SPEC,
        compiler_params=PARAMS,
        name="gather",
    )(share.reshape(1).astype(jnp.int32), *pieces)


def after(value, *others):
    return lax.optimization_barrier((value, *others))[0]


def near_plan(factors, amplitudes, block_list, owner_map):
    pairs = lax.axis_size("pair")
    shares = lax.axis_size("aux")
    wide = shares // 2
    me = lax.axis_index("pair")
    share = lax.axis_index("aux")
    half, part = share & 1, share >> 1
    place = jnp.stack([me, half]).astype(jnp.int32)
    slots, width, depth = amplitudes.shape
    rows = width // 2
    total = pairs * slots
    virt = factors.shape[2]
    factors = factors[0]
    full_rows = factors.shape[0] // FULL
    full_chunk = full_rows // pairs
    chunk = (factors.shape[0] - full_rows) // MEMBERS

    def over_pair(value, distance):
        if distance == 0:
            return value
        return lax.ppermute(value, "pair", [(i, i ^ distance) for i in range(pairs)])

    def over_aux(value, distance):
        return lax.ppermute(value, "aux", [(i, i ^ distance) for i in range(shares)])

    def over_both(value, far, near):
        route = [
            (i * shares + k, (i ^ far) * shares + (k ^ near))
            for i in range(pairs)
            for k in range(shares)
        ]
        return lax.ppermute(value, ("pair", "aux"), route)

    full = factors[:full_rows].reshape(pairs, full_chunk, virt, depth)
    full, turn = lax.optimization_barrier((full, me))
    starts = [full_rows + ((turn & (MEMBERS - 1)) ^ d) * chunk for d in range(MEMBERS)]
    pieces = [lax.dynamic_slice_in_dim(factors, start, chunk, 0) for start in starts]
    pieces = [jnp.transpose(piece, (1, 0, 2)) for piece in pieces]

    packed = pack(place, block_list, owner_map, after(amplitudes, turn))
    near = jnp.stack([over_pair(packed, 2 * i) for i in range(pairs // 2)])
    blocks = jnp.concatenate([near, over_pair(near, 1)])
    meta = blocks[:, slots * rows : slots * rows + slots, :3].astype(jnp.int32)
    listed = plan(meta.reshape(total, 3), slots, pairs, virt)

    full = lax.all_to_all(touch([jnp.transpose(full, (0, 2, 1, 3))], near)[0], "pair", 0, 0, tiled=True)
    for d in (1, 2):
        pieces[d] = after(pieces[d], near)

    others = over_aux(blocks, 1)
    mine = [over_pair(pieces[d], d) for d in range(1, MEMBERS)]
    mine = [pieces[0], *touch(mine, listed, others)]
    own, same, cross, again, stack = contract(place, listed, blocks, others, mine, pairs, virt, rows)
    got = over_pair(same, MEMBERS), over_both(cross, MEMBERS, 1)
    own = own, over_aux(again, 1)
    work = list(zip(own, got, (mine, [over_aux(stack, 1)])))
    full = after(full, same).reshape(pairs * virt, full_chunk, depth)
    out = None
    for held in (full, over_aux(full, 1)):
        out = whole(listed, blocks, held, out, pairs, virt, rows, total)
    for own, got, held in work:
        out = project(place, listed, own, got, held, out, pairs)

    quarter = rows // wide
    out = out[:total].reshape(2, pairs // 2, slots, wide, quarter, depth)
    summed = None
    for h in range(wide):
        piece = lax.dynamic_index_in_dim(out, part ^ h, 3, False)
        for y in range(2):
            value = piece[y]
            if (y, h) != (0, 0):
                value = over_both(value.astype(jnp.bfloat16), y, 2 * h).astype(jnp.float32)
            summed = value if summed is None else summed + value
    summed = summed.astype(jnp.bfloat16)
    home = None
    for i in range(pairs // 2):
        value = over_pair(summed[i], 2 * i).astype(jnp.float32)
        home = value if home is None else home + value
    result = home.astype(jnp.bfloat16)
    return gather(share, [result] + [over_aux(result, a) for a in range(1, shares)])


def far_plan(factors, amplitudes, block_list, owner_map):
    pair_count = lax.axis_size("pair")
    slot_total = pair_count * CAP
    block_count = amplitudes.shape[0]
    block_width = amplitudes.shape[1]
    virt_blocks = factors.shape[2]
    share_rows = factors.shape[1]
    orbital_total = owner_map.shape[0]
    orbitals = block_list[:, 0]
    block_a = block_list[:, 1]
    block_c = block_list[:, 2]
    matches = orbitals[:, None] == lax.iota(jnp.int32, orbital_total)[None, :]
    owners = jnp.sum(jnp.where(matches, owner_map[None, :], 0), axis=1)
    owner_hits = (owners[:, None] == lax.iota(jnp.int32, pair_count)[None, :]).astype(jnp.int32)
    earlier = jnp.cumsum(owner_hits, axis=0) - owner_hits
    slot_rank = jnp.sum(earlier * owner_hits, axis=1)
    slots = owners * CAP + slot_rank
    placing = slots[:, None] == lax.iota(jnp.int32, slot_total)[None, :]
    place_matrix = placing.astype(jnp.bfloat16)
    flat_blocks = amplitudes.reshape(block_count, block_width * block_width)
    send_blocks = jnp.einsum(
        "js,jm->sm", place_matrix, flat_blocks, preferred_element_type=jnp.float32
    )
    send_blocks = send_blocks.astype(jnp.bfloat16).reshape(
        pair_count, CAP, block_width, block_width
    )
    send_a = jnp.sum(jnp.where(placing, block_a[:, None] + 1, 0), axis=0)
    send_c = jnp.sum(jnp.where(placing, block_c[:, None] + 1, 0), axis=0)
    send_index = (
        jnp.stack([send_a, send_c], axis=-1).astype(jnp.bfloat16).reshape(pair_count, CAP, 2)
    )
    recv_blocks, recv_index = (
        lax.all_to_all(send_blocks, "pair", split_axis=0, concat_axis=0, tiled=True),
        lax.all_to_all(send_index, "pair", split_axis=0, concat_axis=0, tiled=True),
    )
    recv_index = recv_index.reshape(slot_total, 2).astype(jnp.int32) - 1
    slot_a = recv_index[:, 0]
    slot_c = recv_index[:, 1]
    onehot_a = (slot_a[:, None] == lax.iota(jnp.int32, virt_blocks)[None, :]).astype(jnp.bfloat16)
    onehot_c = (slot_c[:, None] == lax.iota(jnp.int32, virt_blocks)[None, :]).astype(jnp.bfloat16)
    combined = (onehot_c[:, :, None] * onehot_a[:, None, :]).reshape(
        slot_total, virt_blocks * virt_blocks
    )
    recv_flat = recv_blocks.reshape(slot_total, block_width * block_width)
    weights = jnp.einsum("sm,sn->mn", combined, recv_flat, preferred_element_type=jnp.float32)
    weights = weights.reshape(virt_blocks, virt_blocks, block_width, block_width)
    weights = jnp.transpose(weights, (0, 3, 1, 2)).reshape(
        virt_blocks * block_width, virt_blocks * block_width
    )
    weights = weights.astype(jnp.bfloat16)
    factor_flat = factors.reshape(share_rows, virt_blocks * block_width)
    factor_rows = factor_flat
    inter_share = lax.psum_scatter(
        jnp.dot(factor_rows, weights, preferred_element_type=jnp.float32),
        "pair",
        scatter_dimension=0,
        tiled=True,
    )
    inter_share = inter_share.astype(jnp.bfloat16)
    shard_rows = lax.all_gather(inter_share, "pair", axis=0, tiled=True)
    height = shard_rows.shape[0]
    factor_rows = factor_flat
    left = shard_rows.reshape(height, virt_blocks, block_width)
    right = factor_rows.reshape(height, virt_blocks, block_width)
    projected = jnp.einsum("qAa,qCc->ACac", left, right, preferred_element_type=jnp.float32)
    safe_a = jnp.maximum(slot_a, 0)
    safe_c = jnp.maximum(slot_c, 0)
    summed = lax.psum(projected, "aux")
    picked = summed[safe_a, safe_c].astype(jnp.bfloat16)
    picked = picked.reshape(pair_count, CAP, block_width, block_width)
    returned = lax.all_to_all(picked, "pair", split_axis=0, concat_axis=0, tiled=True)
    returned = returned.reshape(slot_total, block_width * block_width)
    result = jnp.einsum("js,sm->jm", place_matrix, returned, preferred_element_type=jnp.float32)
    return result.astype(jnp.bfloat16).reshape(block_count, block_width, block_width)


def on_device(factors, amplitudes, block_list, owner_map):
    fits = amplitudes.shape[0] < META and factors.shape[2] < META
    plan_of = near_plan if lax.axis_size("pair") == 2 * MEMBERS and fits else far_plan
    return plan_of(factors, amplitudes, block_list, owner_map)


def solution(mesh):
    placed = (P("pair", "aux", None, None), P("pair", None, None), P("pair", None), P())
    return jax.shard_map(
        on_device, mesh=mesh, in_specs=placed, out_specs=P("pair", None, None), check_vma=False
    )
```

```python
import jax
import jax.numpy as jnp
from jax import lax
from jax.experimental import pallas as pl
from jax.experimental.pallas import tpu as pltpu
from jax.sharding import PartitionSpec as P

CAP = 2
BATCH = 6
META = 16
MEMBERS = 4
FULL = 2
VMEM_BYTES = 16 * 1024 * 1024

SMEM_SPEC = pl.BlockSpec(memory_space=pltpu.SMEM)
VMEM_SPEC = pl.BlockSpec(memory_space=pltpu.VMEM)
PARAMS = pltpu.CompilerParams(vmem_limit_bytes=VMEM_BYTES)
COSTS = dict(pack=0, plan=10**13, contract=10**13, whole=0, project=0)


def cost(name):
    return pl.CostEstimate(flops=COSTS[name], bytes_accessed=0, transcendentals=0)


def pack_kernel(place_ref, list_ref, owner_ref, blocks_ref, out_ref):
    half = place_ref[1]
    count, width, depth = blocks_ref.shape
    rows = width // 2
    line = lax.broadcasted_iota(jnp.int32, (META, depth), 0)
    lane = lax.broadcasted_iota(jnp.int32, (META, depth), 1)
    meta = jnp.zeros((META, depth), jnp.float32)
    taken = pl.ds(pl.multiple_of(half * rows, rows), rows)
    for j in range(count):
        out_ref[j * rows : (j + 1) * rows, :] = blocks_ref[j, taken, :]
        owner = owner_ref[list_ref[j, 0]]
        for k, value in enumerate((list_ref[j, 1], list_ref[j, 2], owner)):
            meta = jnp.where((line == j) & (lane == k), value.astype(jnp.float32), meta)
    out_ref[pl.ds(count * rows, META), :] = meta.astype(out_ref.dtype)


def pack(place, block_list, owner_map, blocks):
    count, width, depth = blocks.shape
    return pl.pallas_call(
        pack_kernel,
        out_shape=jax.ShapeDtypeStruct((count * (width // 2) + META, depth), blocks.dtype),
        in_specs=[SMEM_SPEC, SMEM_SPEC, SMEM_SPEC, VMEM_SPEC],
        out_specs=VMEM_SPEC,
        compiler_params=PARAMS,
        cost_estimate=cost("pack"),
        name="pack",
    )(place, block_list, owner_map, blocks)


def plan_kernel(slots, owners, virt, meta_ref, out_ref, filled_ref):
    total = meta_ref.shape[0]
    room = total + BATCH
    for m in range(owners):
        filled_ref[m] = m * room

    def one(s, place):
        owner = meta_ref[s, 2]
        sender, first = place
        where = meta_ref[s, 0] * 16 + meta_ref[s, 1]
        at = filled_ref[owner]
        out_ref[at] = ((s * 16 + sender) * 16 + s - first) * 256 + where
        filled_ref[owner] = at + 1
        over = s + 1 - first == slots
        return sender + over.astype(jnp.int32), jnp.where(over, s + 1, first)

    lax.fori_loop(0, total, one, (jnp.int32(0), jnp.int32(0)))
    for m in range(owners):
        n = filled_ref[m]
        for u in range(BATCH):
            out_ref[n + u] = jnp.int32(total * 65536 + virt * 16)
        out_ref[owners * room + m] = lax.div(n - m * room + BATCH - 1, BATCH)


def plan(meta, slots, owners, virt):
    room = meta.shape[0] + BATCH
    return pl.pallas_call(
        lambda *refs: plan_kernel(slots, owners, virt, *refs),
        out_shape=jax.ShapeDtypeStruct((owners * room + owners,), jnp.int32),
        in_specs=[SMEM_SPEC],
        out_specs=SMEM_SPEC,
        scratch_shapes=[pltpu.SMEM((owners,), jnp.int32)],
        cost_estimate=cost("plan"),
        name="plan",
    )(meta)


def over_slots(plan_ref, owners, picks, step):
    room = plan_ref.shape[0] // owners - 1
    for owner, ref in picks:

        def batch(b, carry, owner=owner, ref=ref):
            step(ref, owner * room + b * BATCH)
            return carry

        lax.fori_loop(0, plan_ref[owners * room + owner], batch, 0)


def add_blocks(plan_ref, blocks_ref, rows, sum_ref):
    def step(factors_ref, first):
        words = [plan_ref[first + i] for i in range(BATCH)]
        terms = []
        for word in words:
            start = pl.multiple_of(((word >> 8) & 15) * rows, rows)
            terms.append(
                lax.dot_general(
                    blocks_ref[(word >> 12) & 15, pl.ds(start, rows), :],
                    factors_ref[word & 15],
                    (((1,), (1,)), ((), ())),
                    preferred_element_type=jnp.float32,
                )
            )
        for word, term in zip(words, terms):
            sum_ref[(word >> 4) & 15] += term

    return step


def add_products(plan_ref, inter_ref, out_ref):
    def step(factors_ref, first):
        words = [plan_ref[first + i] for i in range(BATCH)]
        terms = []
        for word in words:
            terms.append(
                jnp.dot(
                    inter_ref[(word >> 4) & 15],
                    factors_ref[word & 15],
                    preferred_element_type=jnp.float32,
                )
            )
        for word, term in zip(words, terms):
            out_ref[word >> 16] += term

    return step


def contract_kernel(owners, rows, place_ref, plan_ref, blocks_ref, others_ref, *refs):
    pieces = refs[:MEMBERS]
    own_ref, same_ref, cross_ref, again_ref, stack_ref, sum_ref, sems = refs[MEMBERS:]
    virt = own_ref.shape[0]
    copies = [
        pltpu.make_async_copy(ref, stack_ref.at[pl.ds(d * virt, virt)], sems.at[d])
        for d, ref in enumerate(pieces)
    ]
    for copy in copies:
        copy.start()
    sum_ref[...] = jnp.zeros_like(sum_ref)

    def step(factors_ref, first):
        words = [plan_ref[first + i] for i in range(BATCH)]
        terms = []
        for word in words:
            start = pl.multiple_of(((word >> 8) & 15) * rows, rows)
            halves = [ref[(word >> 12) & 15, pl.ds(start, rows), :] for ref in (blocks_ref, others_ref)]
            terms.append(
                lax.dot_general(
                    jnp.concatenate(halves),
                    factors_ref[word & 15],
                    (((1,), (1,)), ((), ())),
                    preferred_element_type=jnp.float32,
                )
            )
        for word, term in zip(words, terms):
            sum_ref[(word >> 4) & 15] += term

    picks = [(place_ref[0] ^ d, ref) for d, ref in enumerate(pieces)]
    over_slots(plan_ref, owners, picks, step)
    own = sum_ref[pl.ds(0, virt), pl.ds(0, rows), :]
    own_ref[...] = own
    same_ref[...] = own.astype(same_ref.dtype)
    cross = sum_ref[pl.ds(0, virt), pl.ds(rows, rows), :].astype(cross_ref.dtype)
    cross_ref[...] = cross
    again_ref[...] = cross
    for copy in copies:
        copy.wait()


def contract(place, listed, blocks, others, factors, owners, virt, rows):
    chunk, depth = factors[0].shape[1:]
    sent = jax.ShapeDtypeStruct((virt, rows, chunk), jnp.bfloat16)
    stack = jax.ShapeDtypeStruct((MEMBERS * virt, chunk, depth), jnp.bfloat16)
    return pl.pallas_call(
        lambda *refs: contract_kernel(owners, rows, *refs),
        out_shape=(jax.ShapeDtypeStruct((virt, rows, chunk), jnp.float32), sent, sent, sent, stack),
        in_specs=[SMEM_SPEC] * 2 + [VMEM_SPEC] * (2 + len(factors)),
        out_specs=(VMEM_SPEC,) * 4 + (pl.BlockSpec(memory_space=pl.ANY),),
        scratch_shapes=[
            pltpu.VMEM((virt + 1, 2 * rows, chunk), jnp.float32),
            pltpu.SemaphoreType.DMA((MEMBERS,)),
        ],
        compiler_params=PARAMS,
        cost_estimate=cost("contract"),
        name="contract",
    )(place, listed, blocks, others, *factors)


def whole_kernel(owners, rows, virt, plan_ref, blocks_ref, *refs):
    out_ref, sum_ref, inter_ref = refs[-3:]
    factors_ref = refs[0]
    so_far = refs[1:-3]
    out_ref[...] = so_far[0][...] if so_far else jnp.zeros_like(out_ref)
    sum_ref[...] = jnp.zeros_like(sum_ref)
    picks = [(k, factors_ref.at[pl.ds(k * virt, virt)]) for k in range(owners)]
    over_slots(plan_ref, owners, picks, add_blocks(plan_ref, blocks_ref, rows, sum_ref))
    inter_ref[...] = sum_ref[...].astype(inter_ref.dtype)
    over_slots(plan_ref, owners, picks, add_products(plan_ref, inter_ref, out_ref))


def whole(listed, blocks, factors, so_far, owners, virt, rows, total):
    chunk, depth = factors.shape[1:]
    so_far = [] if so_far is None else [so_far]
    return pl.pallas_call(
        lambda *refs: whole_kernel(owners, rows, virt, *refs),
        out_shape=jax.ShapeDtypeStruct((total + 1, rows, depth), jnp.float32),
        in_specs=[SMEM_SPEC] + [VMEM_SPEC] * (2 + len(so_far)),
        out_specs=VMEM_SPEC,
        scratch_shapes=[
            pltpu.VMEM((virt + 1, rows, chunk), jnp.float32),
            pltpu.VMEM((virt + 1, rows, chunk), jnp.bfloat16),
        ],
        compiler_params=PARAMS,
        cost_estimate=cost("whole"),
        name="whole",
    )(listed, blocks, factors, *so_far)


def project_kernel(owners, place_ref, plan_ref, own_ref, got_ref, so_far_ref, *refs):
    out_ref, inter_ref = refs[-2:]
    virt = got_ref.shape[0]
    summed = own_ref[...].astype(jnp.float32) + got_ref[...].astype(jnp.float32)
    inter_ref[pl.ds(0, virt)] = summed.astype(inter_ref.dtype)
    inter_ref[virt] = jnp.zeros(inter_ref.shape[1:], inter_ref.dtype)
    out_ref[...] = so_far_ref[...]
    pieces = refs[:-2]
    if len(pieces) == 1:
        pieces = [refs[0].at[pl.ds(d * virt, virt)] for d in range(MEMBERS)]
    picks = [(place_ref[0] ^ d, ref) for d, ref in enumerate(pieces)]
    over_slots(plan_ref, owners, picks, add_products(plan_ref, inter_ref, out_ref))


def project(place, listed, own, got, factors, so_far, owners):
    virt, rows, chunk = got.shape
    return pl.pallas_call(
        lambda *refs: project_kernel(owners, *refs),
        out_shape=jax.ShapeDtypeStruct(so_far.shape, jnp.float32),
        in_specs=[SMEM_SPEC] * 2 + [VMEM_SPEC] * (3 + len(factors)),
        out_specs=VMEM_SPEC,
        scratch_shapes=[pltpu.VMEM((virt + 1, rows, chunk), jnp.bfloat16)],
        compiler_params=PARAMS,
        cost_estimate=cost("project"),
        name="project",
    )(place, listed, own, got, so_far, *factors)


def touch(values, *others):
    values = list(values)
    anywhere = pl.BlockSpec(memory_space=pl.ANY)
    return pl.pallas_call(
        lambda *refs: None,
        out_shape=[jax.ShapeDtypeStruct(value.shape, value.dtype) for value in values],
        in_specs=[anywhere] * (len(values) + len(others)),
        out_specs=[anywhere] * len(values),
        input_output_aliases={i: i for i in range(len(values))},
        name="touch",
    )(*values, *others)


def gather_kernel(place_ref, *refs):
    out_ref = refs[-1]
    shares = len(refs) - 1
    rows = out_ref.shape[1] // shares
    for a, ref in enumerate(refs[:-1]):
        share = place_ref[0] ^ a
        start = ((share & 1) * (shares // 2) + (share >> 1)) * rows
        out_ref[:, pl.ds(pl.multiple_of(start, rows), rows), :] = ref[...]


def gather(share, pieces):
    slots, rows, depth = pieces[0].shape
    return pl.pallas_call(
        gather_kernel,
        out_shape=jax.ShapeDtypeStruct((slots, rows * len(pieces), depth), pieces[0].dtype),
        in_specs=[SMEM_SPEC] + [VMEM_SPEC] * len(pieces),
        out_specs=VMEM_SPEC,
        compiler_params=PARAMS,
        name="gather",
    )(share.reshape(1).astype(jnp.int32), *pieces)


def after(value, *others):
    return lax.optimization_barrier((value, *others))[0]


def near_plan(factors, amplitudes, block_list, owner_map):
    pairs = lax.axis_size("pair")
    shares = lax.axis_size("aux")
    wide = shares // 2
    me = lax.axis_index("pair")
    share = lax.axis_index("aux")
    half, part = share & 1, share >> 1
    place = jnp.stack([me, half]).astype(jnp.int32)
    slots, width, depth = amplitudes.shape
    rows = width // 2
    total = pairs * slots
    virt = factors.shape[2]
    factors = factors[0]
    full_rows = factors.shape[0] // FULL
    full_chunk = full_rows // pairs
    chunk = (factors.shape[0] - full_rows) // MEMBERS

    def over_pair(value, distance):
        if distance == 0:
            return value
        return lax.ppermute(value, "pair", [(i, i ^ distance) for i in range(pairs)])

    def over_aux(value, distance):
        return lax.ppermute(value, "aux", [(i, i ^ distance) for i in range(shares)])

    def over_both(value, far, near):
        route = [
            (i * shares + k, (i ^ far) * shares + (k ^ near))
            for i in range(pairs)
            for k in range(shares)
        ]
        return lax.ppermute(value, ("pair", "aux"), route)

    full = factors[:full_rows].reshape(pairs, full_chunk, virt, depth)
    full, turn = lax.optimization_barrier((full, me))
    starts = [full_rows + ((turn & (MEMBERS - 1)) ^ d) * chunk for d in range(MEMBERS)]
    pieces = [lax.dynamic_slice_in_dim(factors, start, chunk, 0) for start in starts]
    pieces = [jnp.transpose(piece, (1, 0, 2)) for piece in pieces]

    packed = pack(place, block_list, owner_map, after(amplitudes, turn))
    near = jnp.stack([over_pair(packed, 2 * i) for i in range(pairs // 2)])
    blocks = jnp.concatenate([near, over_pair(near, 1)])
    meta = blocks[:, slots * rows : slots * rows + slots, :3].astype(jnp.int32)
    listed = plan(meta.reshape(total, 3), slots, pairs, virt)

    full = lax.all_to_all(touch([jnp.transpose(full, (0, 2, 1, 3))], near)[0], "pair", 0, 0, tiled=True)
    for d in (1, 2):
        pieces[d] = after(pieces[d], near)

    others = over_aux(blocks, 1)
    mine = [over_pair(pieces[d], d) for d in range(1, MEMBERS)]
    mine = [pieces[0], *touch(mine, listed)]
    own, same, cross, again, stack = contract(place, listed, blocks, others, mine, pairs, virt, rows)
    got = over_pair(same, MEMBERS), over_both(cross, MEMBERS, 1)
    own = own, over_aux(again, 1)
    work = list(zip(own, got, (mine, [over_aux(stack, 1)])))
    full = after(full, same).reshape(pairs * virt, full_chunk, depth)
    out = None
    for held in (full, over_aux(full, 1)):
        out = whole(listed, blocks, held, out, pairs, virt, rows, total)
    for own, got, held in work:
        out = project(place, listed, own, got, held, out, pairs)

    quarter = rows // wide
    out = out[:total].reshape(2, pairs // 2, slots, wide, quarter, depth)
    summed = None
    for h in range(wide):
        piece = lax.dynamic_index_in_dim(out, part ^ h, 3, False)
        for y in range(2):
            value = piece[y]
            if (y, h) != (0, 0):
                value = over_both(value.astype(jnp.bfloat16), y, 2 * h).astype(jnp.float32)
            summed = value if summed is None else summed + value
    summed = summed.astype(jnp.bfloat16)
    home = None
    for i in range(pairs // 2):
        value = over_pair(summed[i], 2 * i).astype(jnp.float32)
        home = value if home is None else home + value
    result = home.astype(jnp.bfloat16)
    return gather(share, [result] + [over_aux(result, a) for a in range(1, shares)])


def far_plan(factors, amplitudes, block_list, owner_map):
    pair_count = lax.axis_size("pair")
    slot_total = pair_count * CAP
    block_count = amplitudes.shape[0]
    block_width = amplitudes.shape[1]
    virt_blocks = factors.shape[2]
    share_rows = factors.shape[1]
    orbital_total = owner_map.shape[0]
    orbitals = block_list[:, 0]
    block_a = block_list[:, 1]
    block_c = block_list[:, 2]
    matches = orbitals[:, None] == lax.iota(jnp.int32, orbital_total)[None, :]
    owners = jnp.sum(jnp.where(matches, owner_map[None, :], 0), axis=1)
    owner_hits = (owners[:, None] == lax.iota(jnp.int32, pair_count)[None, :]).astype(jnp.int32)
    earlier = jnp.cumsum(owner_hits, axis=0) - owner_hits
    slot_rank = jnp.sum(earlier * owner_hits, axis=1)
    slots = owners * CAP + slot_rank
    placing = slots[:, None] == lax.iota(jnp.int32, slot_total)[None, :]
    place_matrix = placing.astype(jnp.bfloat16)
    flat_blocks = amplitudes.reshape(block_count, block_width * block_width)
    send_blocks = jnp.einsum(
        "js,jm->sm", place_matrix, flat_blocks, preferred_element_type=jnp.float32
    )
    send_blocks = send_blocks.astype(jnp.bfloat16).reshape(
        pair_count, CAP, block_width, block_width
    )
    send_a = jnp.sum(jnp.where(placing, block_a[:, None] + 1, 0), axis=0)
    send_c = jnp.sum(jnp.where(placing, block_c[:, None] + 1, 0), axis=0)
    send_index = (
        jnp.stack([send_a, send_c], axis=-1).astype(jnp.bfloat16).reshape(pair_count, CAP, 2)
    )
    recv_blocks, recv_index = (
        lax.all_to_all(send_blocks, "pair", split_axis=0, concat_axis=0, tiled=True),
        lax.all_to_all(send_index, "pair", split_axis=0, concat_axis=0, tiled=True),
    )
    recv_index = recv_index.reshape(slot_total, 2).astype(jnp.int32) - 1
    slot_a = recv_index[:, 0]
    slot_c = recv_index[:, 1]
    onehot_a = (slot_a[:, None] == lax.iota(jnp.int32, virt_blocks)[None, :]).astype(jnp.bfloat16)
    onehot_c = (slot_c[:, None] == lax.iota(jnp.int32, virt_blocks)[None, :]).astype(jnp.bfloat16)
    combined = (onehot_c[:, :, None] * onehot_a[:, None, :]).reshape(
        slot_total, virt_blocks * virt_blocks
    )
    recv_flat = recv_blocks.reshape(slot_total, block_width * block_width)
    weights = jnp.einsum("sm,sn->mn", combined, recv_flat, preferred_element_type=jnp.float32)
    weights = weights.reshape(virt_blocks, virt_blocks, block_width, block_width)
    weights = jnp.transpose(weights, (0, 3, 1, 2)).reshape(
        virt_blocks * block_width, virt_blocks * block_width
    )
    weights = weights.astype(jnp.bfloat16)
    factor_flat = factors.reshape(share_rows, virt_blocks * block_width)
    factor_rows = factor_flat
    inter_share = lax.psum_scatter(
        jnp.dot(factor_rows, weights, preferred_element_type=jnp.float32),
        "pair",
        scatter_dimension=0,
        tiled=True,
    )
    inter_share = inter_share.astype(jnp.bfloat16)
    shard_rows = lax.all_gather(inter_share, "pair", axis=0, tiled=True)
    height = shard_rows.shape[0]
    factor_rows = factor_flat
    left = shard_rows.reshape(height, virt_blocks, block_width)
    right = factor_rows.reshape(height, virt_blocks, block_width)
    projected = jnp.einsum("qAa,qCc->ACac", left, right, preferred_element_type=jnp.float32)
    safe_a = jnp.maximum(slot_a, 0)
    safe_c = jnp.maximum(slot_c, 0)
    summed = lax.psum(projected, "aux")
    picked = summed[safe_a, safe_c].astype(jnp.bfloat16)
    picked = picked.reshape(pair_count, CAP, block_width, block_width)
    returned = lax.all_to_all(picked, "pair", split_axis=0, concat_axis=0, tiled=True)
    returned = returned.reshape(slot_total, block_width * block_width)
    result = jnp.einsum("js,sm->jm", place_matrix, returned, preferred_element_type=jnp.float32)
    return result.astype(jnp.bfloat16).reshape(block_count, block_width, block_width)


def on_device(factors, amplitudes, block_list, owner_map):
    fits = amplitudes.shape[0] < META and factors.shape[2] < META
    plan_of = near_plan if lax.axis_size("pair") == 2 * MEMBERS and fits else far_plan
    return plan_of(factors, amplitudes, block_list, owner_map)


def solution(mesh):
    placed = (P("pair", "aux", None, None), P("pair", None, None), P("pair", None), P())
    return jax.shard_map(
        on_device, mesh=mesh, in_specs=placed, out_specs=P("pair", None, None), check_vma=False
    )
```
